32 devices in a mesh: row: 8 (over z, core), col: 4 (over y, x).
Axes of the slice: x: 2, y: 2, z: 4, core: 2. Of those that a mesh axis runs over, the one named last changes fastest.
Arguments:
- features: bfloat16 [8192, 128], P(('col', 'row')), may hold values from -96 to 96
- weight: bfloat16 [128, 256], replicated, may hold values from -0.5 to 0.5
- bias: float32 [256], replicated, may hold values from -3 to 3
- cotangent: bfloat16 [8192, 256], P(('row', 'col')), may hold values from -6 to 6
- tile_values: bfloat16 [8, 4, 128, 128, 128], P('row', 'col'), may hold values from 0 to 4, as said below
- tile_pos: int32 [8, 4, 2, 128], P('row', 'col'), may hold values from 0 to 15, as said below
- tile_count: int32 [8, 4], P('row', 'col'), may hold values from 0 to 128, as said below
- block_perm: int32 [64], replicated, may hold values from 0 to 63, as said below
Outputs:
- hidden: bfloat16 [8192, 256], P(('row', 'col'))
- weight_grad: float32 [128, 256], replicated
- bias_grad: float32 [256], replicated
The draws below stay inside these ranges and needn't reach their ends.
Inputs may be any that keep to these rules, and one draw needn't show every extreme that they name: `tile_values`: entries are 0 or a weight of at least 0.25; slots t at or beyond tile_count[r, c] belong to no tile. `tile_pos`: entry [r, c, 0, t] is the slot's tile row, below 8, within row block r, and [r, c, 1, t] its tile column, below 16, within column block c, both in the reordered numbering; the slots of one cell hold distinct positions. `tile_count`: every draw has a cell with 128 live slots. `block_perm`: each aligned run of 8 entries is a permutation of that run's own indices.
All inputs are finite; a program needn't handle non-finite values.
Results may differ from the reference program's by a relative error of at most 0.0059.
Values may be sent and summed in bfloat16 or wider, within the bound.
A program may use at most 64 MiB of HBM per device.

```python
import jax
import jax.numpy as jnp
from jax import lax

TILE = 128
FEAT = 128
HIDDEN_SIZE = 256
ROW_TILES = 8
ROW_BLOCKS = 8
COL_BLOCKS = 4
COL_TILES = 16
MAX_TILES = 128
NODES = 8192


def draw_tile_values(key, part):
    shape = (ROW_BLOCKS, COL_BLOCKS, MAX_TILES, TILE, TILE)
    key_mask, key_level, key_cell = jax.random.split(jax.random.fold_in(key, 11), 3)
    cell_density = jnp.exp(jax.random.uniform(key_cell, (ROW_BLOCKS, COL_BLOCKS, 1, 1, 1), jnp.float32, -2.1202635, 0.0))
    chance = jax.random.uniform(key_mask, shape, jnp.float32, 0.0, 1.0)
    present = (chance < cell_density).astype(jnp.float32)
    levels = jax.random.uniform(key_level, shape, jnp.float32, -1.3862944, 1.3862944)
    return (present * jnp.exp(levels)).astype(jnp.bfloat16)


def draw_tile_pos(key, part):
    cell_keys = jax.random.split(jax.random.fold_in(key, 23), ROW_BLOCKS * COL_BLOCKS)
    positions = jax.vmap(lambda single: jax.random.permutation(single, MAX_TILES))(cell_keys).astype(jnp.int32)
    tile_rows = positions // COL_TILES
    tile_cols = positions % COL_TILES
    stacked = jnp.stack([tile_rows, tile_cols], axis=1)
    return stacked.reshape(ROW_BLOCKS, COL_BLOCKS, 2, MAX_TILES)


def draw_tile_count(key, part):
    key_one, key_two, key_three = jax.random.split(jax.random.fold_in(key, 37), 3)
    cell_total = ROW_BLOCKS * COL_BLOCKS
    first_draw = jax.random.randint(key_one, (cell_total,), 1, MAX_TILES + 1, dtype=jnp.int32)
    second_draw = jax.random.randint(key_two, (cell_total,), 1, MAX_TILES + 1, dtype=jnp.int32)
    counts = first_draw * second_draw // MAX_TILES
    busiest = jax.random.randint(key_three, (), 0, cell_total, dtype=jnp.int32)
    counts = jnp.where(jnp.arange(cell_total, dtype=jnp.int32) == busiest, MAX_TILES, counts)
    return counts.reshape(ROW_BLOCKS, COL_BLOCKS).astype(jnp.int32)


def draw_block_perm(key, part):
    block_keys = jax.random.split(jax.random.fold_in(key, 41), ROW_BLOCKS)
    local_order = jax.vmap(lambda single: jax.random.permutation(single, ROW_TILES))(block_keys).astype(jnp.int32)
    offsets = (jnp.arange(ROW_BLOCKS, dtype=jnp.int32) * ROW_TILES)[:, None]
    return (local_order + offsets).reshape(ROW_BLOCKS * ROW_TILES)


def steps_of(own_key, dims, cuts, low, largest):
    level, own = 1.0, jax.random.fold_in(own_key, 6)
    for position, shards_of in cuts:
        heights = jnp.exp(jax.random.uniform(jax.random.fold_in(own, position), (shards_of,), jnp.float32, low / len(cuts), largest / len(cuts)))
        level = level * jnp.repeat(heights, dims[position] // shards_of).reshape([-1 if axis == position else 1 for axis in range(len(dims))])
    return level


def bell_draw(rng, extent, deviation, bound, shards=(), kind=jnp.bfloat16):
    drawn = deviation * jax.random.normal(rng, extent, jnp.float32)
    if shards:
        drawn = drawn * steps_of(rng, extent, shards, -0.22, 0.18)
    return jnp.clip(drawn, -bound, bound).astype(kind)


def setup_inputs(seed: int = 0) -> dict:
    key_list = jax.random.split(jax.random.key(seed), 9)
    return {
        "features": bell_draw(key_list[0], (NODES, FEAT), 16.0, 96.0, ((0, 32),)),
        "weight": bell_draw(key_list[1], (FEAT, HIDDEN_SIZE), FEAT ** -0.5, 0.5),
        "bias": bell_draw(key_list[2], (HIDDEN_SIZE,), 0.5, 3.0, (), jnp.float32),
        "cotangent": bell_draw(key_list[3], (NODES, HIDDEN_SIZE), 1.0, 6.0, ((0, 32),)),
        "tile_values": draw_tile_values(jax.random.fold_in(key_list[8], 71), 0),
        "tile_pos": draw_tile_pos(jax.random.fold_in(key_list[8], 71), 0),
        "tile_count": draw_tile_count(jax.random.fold_in(key_list[8], 71), 0),
        "block_perm": draw_block_perm(jax.random.fold_in(key_list[8], 71), 0),
    }


def reference(features, weight, bias, cotangent, tile_values, tile_pos, tile_count, block_perm):
    slot_index = jnp.arange(MAX_TILES, dtype=jnp.int32)

    def cell_maps(row_block, col_block):
        positions = tile_pos[row_block, col_block]
        row_local = block_perm[row_block * ROW_TILES + positions[0]] - row_block * ROW_TILES
        col_local = block_perm[col_block * COL_TILES + positions[1]] - col_block * COL_TILES
        is_live = slot_index < tile_count[row_block, col_block]
        return (row_local, col_local, is_live)

    def degree_cell(cell_index):
        row_block = cell_index // COL_BLOCKS
        col_block = cell_index % COL_BLOCKS
        row_local, col_local, is_live = cell_maps(row_block, col_block)
        values = tile_values[row_block, col_block].astype(jnp.float32)
        row_part = lax.optimization_barrier(jnp.sum(values, axis=2))
        col_part = lax.optimization_barrier(jnp.sum(values, axis=1))
        row_part = jnp.where(is_live[:, None], row_part, 0.0).astype(jnp.float32)
        col_part = jnp.where(is_live[:, None], col_part, 0.0).astype(jnp.float32)
        row_sums = jnp.zeros((ROW_TILES, TILE), jnp.float32).at[row_local].add(row_part)
        col_sums = jnp.zeros((COL_TILES, TILE), jnp.float32).at[col_local].add(col_part)
        return (row_sums.reshape(ROW_TILES * TILE), col_sums.reshape(COL_TILES * TILE))
    cells = jnp.arange(ROW_BLOCKS * COL_BLOCKS, dtype=jnp.int32)
    row_sums, col_sums = lax.map(degree_cell, cells)
    row_degree = 1.0 + lax.optimization_barrier(jnp.sum(row_sums.reshape(ROW_BLOCKS, COL_BLOCKS, ROW_TILES * TILE), axis=1)).reshape(NODES)
    col_degree = 1.0 + lax.optimization_barrier(jnp.sum(col_sums.reshape(ROW_BLOCKS, COL_BLOCKS, COL_TILES * TILE), axis=0)).reshape(NODES)
    scaled = (lax.rsqrt(col_degree)[:, None] * features.astype(jnp.float32)).astype(jnp.bfloat16)

    def row_product(row_block):

        def cell_step(running, col_block):
            row_local, col_local, is_live = cell_maps(row_block, col_block)
            values = tile_values[row_block, col_block].astype(jnp.float32)
            values = values * is_live[:, None, None].astype(jnp.float32)
            dense_cell = jnp.zeros((ROW_TILES, COL_TILES, TILE, TILE), jnp.float32).at[row_local, col_local].add(values)
            dense_cell = jnp.transpose(dense_cell, (0, 2, 1, 3)).reshape(ROW_TILES * TILE, COL_TILES * TILE)
            inputs = lax.dynamic_slice_in_dim(scaled, col_block * (COL_TILES * TILE), COL_TILES * TILE, 0).astype(jnp.float32)
            product = jnp.dot(dense_cell, inputs, preferred_element_type=jnp.float32, precision=lax.Precision.HIGHEST)
            return (running + product, None)
        running, _ = lax.scan(cell_step, jnp.zeros((ROW_TILES * TILE, FEAT), jnp.float32), jnp.arange(COL_BLOCKS, dtype=jnp.int32))
        return running
    summed = lax.map(row_product, jnp.arange(ROW_BLOCKS, dtype=jnp.int32)).reshape(NODES, FEAT)
    aggregated = (lax.rsqrt(row_degree)[:, None] * summed).astype(jnp.bfloat16)
    preact = jnp.dot(aggregated, weight, preferred_element_type=jnp.float32) + bias
    logistic = jax.nn.sigmoid(preact)
    hidden = (preact * logistic).astype(jnp.bfloat16)
    preact_grad = (cotangent.astype(jnp.float32) * logistic * (1.0 + preact * (1.0 - logistic))).astype(jnp.bfloat16)
    inverse_root = lax.rsqrt(jnp.float32(NODES))
    weight_grad = jnp.dot(aggregated.T, preact_grad, preferred_element_type=jnp.float32) * inverse_root
    bias_grad = lax.optimization_barrier(jnp.sum(preact_grad.astype(jnp.float32), axis=0)) * inverse_root
    return (hidden, weight_grad, bias_grad)
```

```python
import functools

import jax
import jax.numpy as jnp
from jax import lax
from jax.experimental import pallas as pl
from jax.experimental.pallas import tpu as pltpu
from jax.sharding import PartitionSpec as P

MESH = pl.DeviceIdType.MESH
F32 = jnp.float32
BF16 = jnp.bfloat16
WIRE = jnp.float32
TILE_ROWS = 8
LANES = 128


def kernel(
    row_count,
    col_count,
    feat_ref,
    weight_ref,
    bias_ref,
    cot_ref,
    tiles_hbm,
    pos_ref,
    count_ref,
    perm_ref,
    hidden_ref,
    wgrad_ref,
    bgrad_ref,
    tiles,
    dense,
    index_vmem,
    index_smem,
    gathered,
    scaled,
    col_buf,
    row_send,
    row_buf,
    prod_send,
    prod_buf,
    grad_send,
    grad_buf,
    out_buf,
    tile_sem,
    index_sem,
    feat_send_sem,
    feat_recv_sem,
    small_send_sem,
    small_recv_sem,
):
    row = lax.axis_index("row")
    col = lax.axis_index("col")
    device_count = row_count * col_count
    me = row * col_count + col
    core = lax.rem(row, 2)
    chip = row // 2
    chips = row_count // 2
    sibling = row + 1 - 2 * core
    max_tiles = tiles.shape[0] - 1
    tile = tiles.shape[1]
    row_tiles = dense.shape[0] // tile
    col_tiles = dense.shape[1] // tile
    own_rows = hidden_ref.shape[0]
    feat_rows, feat_width = feat_ref.shape
    hidden_width = weight_ref.shape[1]
    grad_tiles = out_buf.shape[0]
    halves = hidden_width // LANES

    tile_copy = pltpu.make_async_copy(
        tiles_hbm.at[0, 0], tiles.at[pl.ds(0, max_tiles)], tile_sem
    )
    tile_copy.start()

    barrier = pltpu.get_barrier_semaphore()

    def greet(step, carry):
        other = lax.rem(me + step, device_count)
        pl.semaphore_signal(
            barrier,
            inc=1,
            device_id=(other // col_count, lax.rem(other, col_count)),
            device_id_type=MESH,
        )
        return carry

    lax.fori_loop(1, device_count, greet, 0)

    tile_row = pos_ref[0, 0, 0:1, :]
    tile_col = pos_ref[0, 0, 1:2, :]
    code_row = jnp.zeros((1, max_tiles), jnp.int32)
    for i in range(row_tiles):
        place = perm_ref[row * row_tiles + i] - row * row_tiles
        code_row = jnp.where(tile_row == i, place, code_row)
    code_col = jnp.zeros((1, max_tiles), jnp.int32)
    for j in range(col_tiles):
        place = perm_ref[col * col_tiles + j] - col * col_tiles
        code_col = jnp.where(tile_col == j, place, code_col)
    slot_lane = lax.broadcasted_iota(jnp.int32, (1, max_tiles), 1)
    code = jnp.where(slot_lane < count_ref[0, 0], code_row * col_tiles + code_col, -1)
    code = jnp.transpose(jnp.broadcast_to(code, (LANES, max_tiles)))
    positions = row_tiles * col_tiles
    slot_sub = lax.broadcasted_iota(jnp.int32, (max_tiles, LANES), 0)
    for start in range(0, positions, LANES):
        place = lax.broadcasted_iota(jnp.int32, (max_tiles, LANES), 1) + start
        slot = jnp.min(jnp.where(code == place, slot_sub, max_tiles), axis=0, keepdims=True)
        index_vmem[:, start : start + LANES] = jnp.broadcast_to(slot, (8, LANES))
    index_copy = pltpu.make_async_copy(index_vmem, index_smem, index_sem)
    index_copy.start()
    tiles[max_tiles] = jnp.zeros((tile, tile), BF16)

    pl.semaphore_wait(barrier, device_count - 1)

    def feat_copy(source, source_row, target_row, send_slot):
        return pltpu.make_async_remote_copy(
            src_ref=source,
            dst_ref=gathered.at[source_row],
            send_sem=feat_send_sem.at[send_slot],
            recv_sem=feat_recv_sem.at[source_row],
            device_id=(target_row, col),
            device_id_type=MESH,
        )

    for step in range(1, chips):
        target = lax.rem(chip + step, chips) * 2 + core
        feat_copy(feat_ref, row, target, step).start()
    feat_copy(feat_ref, row, sibling, 0).start()
    gathered[row] = feat_ref[...]

    tile_copy.wait()
    index_copy.wait()

    def build(b, carry):
        columns = pl.ds(pl.multiple_of(b * tile, tile), tile)
        total = jnp.zeros((tile, tile), F32)
        for a in range(row_tiles):
            block = tiles[index_smem[0, a * col_tiles + b]]
            dense[a * tile : (a + 1) * tile, columns] = block
            total = total + block.astype(F32)
        col_buf[row, pl.ds(b, 1), :] = jnp.sum(total, axis=0, keepdims=True)
        return carry

    lax.fori_loop(0, col_tiles, build, 0)

    def small_copy(source, target_ref, target_row, target_col, which):
        return pltpu.make_async_remote_copy(
            src_ref=source,
            dst_ref=target_ref,
            send_sem=small_send_sem.at[which],
            recv_sem=small_recv_sem.at[which],
            device_id=(target_row, target_col),
            device_id_type=MESH,
        )

    def wait_all(source, target_ref, which):
        copy = small_copy(source, target_ref, sibling, col, which)
        copy.wait_send()
        copy.wait_recv()

    for step in range(1, row_count):
        target = lax.rem(row + step, row_count)
        small_copy(col_buf.at[row], col_buf.at[row], target, col, 0).start()

    ones = jnp.ones((dense.shape[1], LANES), BF16)
    for k in range(col_count):
        for piece in range(own_rows // tile):
            at = k * own_rows + piece * tile
            sums = jnp.dot(dense[at : at + tile, :], ones, preferred_element_type=F32)
            row_send[k, :, piece * tile : (piece + 1) * tile] = jnp.transpose(sums)[0:8, :]
    for step in range(1, col_count):
        target = lax.rem(col + step, col_count)
        small_copy(row_send.at[target], row_buf.at[col], row, target, 1).start()
    row_buf[col] = row_send[col]

    for step in range(1, chips):
        source = lax.rem(chip + chips - step, chips) * 2 + core
        feat_copy(feat_ref, source, sibling, 0).wait_recv()
        feat_copy(gathered.at[source], source, sibling, chips + step - 1).start()

    wait_all(col_buf.at[pl.ds(0, row_count - 1)], col_buf.at[pl.ds(0, row_count - 1)], 0)
    col_total = col_buf[0]
    for r in range(1, row_count):
        col_total = col_total + col_buf[r]
    col_scale = lax.rsqrt(1.0 + col_total)
    col_scale = jnp.concatenate(
        [col_scale, jnp.zeros((LANES - col_tiles, tile), F32)], axis=0
    )
    col_scale = jnp.transpose(col_scale)

    wait_all(row_buf.at[pl.ds(0, col_count - 1)], row_buf.at[pl.ds(0, col_count - 1)], 1)
    row_total = row_buf[0]
    for c in range(1, col_count):
        row_total = row_total + row_buf[c]
    row_scale = lax.rsqrt(1.0 + row_total)
    row_scale = jnp.concatenate(
        [
            jnp.transpose(
                jnp.broadcast_to(row_scale[0:1, at : at + tile], (LANES, tile))
            )
            for at in range(0, own_rows, tile)
        ],
        axis=0,
    )

    feat_copy(feat_ref, sibling, sibling, 0).wait_recv()
    for step in range(1, chips):
        source = lax.rem(chip + chips - step, chips) * 2 + 1 - core
        feat_copy(feat_ref, source, sibling, 0).wait_recv()
    per_device = feat_rows // tile
    for j in range(col_tiles):
        at = (j % per_device) * tile
        block = gathered[j // per_device, at : at + tile, :].astype(F32)
        scaled[j * tile : (j + 1) * tile, :] = (col_scale[:, j : j + 1] * block).astype(BF16)

    def product(piece):
        rows = pl.ds(pl.multiple_of(piece * own_rows, own_rows), own_rows)
        return jnp.dot(dense[rows, :], scaled[...], preferred_element_type=F32)

    for step in range(1, col_count):
        target = lax.rem(col + step, col_count)
        prod_send[step - 1] = product(target).astype(WIRE)
        small_copy(prod_send.at[step - 1], prod_buf.at[col], row, target, 2).start()
    summed = product(col)
    prod_buf[col] = jnp.zeros((own_rows, feat_width), WIRE)
    wait_all(prod_send, prod_buf.at[pl.ds(0, col_count - 1)], 2)
    for c in range(col_count):
        summed = summed + prod_buf[c].astype(F32)

    aggregated = (row_scale * summed).astype(BF16)
    preact = jnp.dot(aggregated, weight_ref[...], preferred_element_type=F32) + bias_ref[...]
    logistic = jax.nn.sigmoid(preact)
    hidden_ref[...] = (preact * logistic).astype(BF16)
    preact_grad = (
        cot_ref[...].astype(F32) * logistic * (1.0 + preact * (1.0 - logistic))
    ).astype(BF16)
    weight_part = lax.dot_general(
        aggregated, preact_grad, (((0,), (0,)), ((), ())), preferred_element_type=F32
    )
    bias_part = jnp.sum(preact_grad.astype(F32), axis=0, keepdims=True)

    bias_rows = jnp.concatenate(
        [bias_part[:, h * LANES : (h + 1) * LANES] for h in range(halves)]
        + [jnp.zeros((TILE_ROWS - halves, LANES), F32)],
        axis=0,
    )
    for t in range(grad_tiles):
        i, h = t // halves, t % halves
        part = weight_part[i * TILE_ROWS : (i + 1) * TILE_ROWS, h * LANES : (h + 1) * LANES]
        grad_send[t] = jnp.concatenate([part, bias_rows], axis=0).astype(BF16)

    def send_part(step, carry):
        other = lax.rem(me + step, device_count)
        small_copy(
            grad_send.at[lax.rem(other, grad_tiles)],
            grad_buf.at[me],
            other // col_count,
            lax.rem(other, col_count),
            3,
        ).start()
        return carry

    lax.fori_loop(1, device_count, send_part, 0)
    own_tile = lax.rem(me, grad_tiles)
    grad_buf[me] = grad_send[own_tile]
    wait_all(
        grad_buf.at[pl.ds(0, device_count - 1)], grad_buf.at[pl.ds(0, device_count - 1)], 3
    )

    def add_part(d, total):
        return total + grad_buf[d].astype(F32)

    total = lax.fori_loop(0, device_count, add_part, jnp.zeros((2 * TILE_ROWS, LANES), F32))
    inverse_root = lax.rsqrt(F32(own_rows * device_count))
    total = total * inverse_root
    out_buf[own_tile] = total[0:TILE_ROWS]
    first = me - own_tile

    def send_total(step, carry):
        other = first + lax.rem(own_tile + step, grad_tiles)
        small_copy(
            out_buf.at[own_tile],
            out_buf.at[own_tile],
            other // col_count,
            lax.rem(other, col_count),
            4,
        ).start()
        return carry

    lax.fori_loop(1, grad_tiles, send_total, 0)
    for h in range(halves):
        bgrad_ref[:, h * LANES : (h + 1) * LANES] = total[TILE_ROWS + h : TILE_ROWS + h + 1]
    for step in range(1, chips):
        feat_copy(feat_ref, row, sibling, step).wait_send()
        feat_copy(feat_ref, row, sibling, chips + step - 1).wait_send()
    feat_copy(feat_ref, row, sibling, 0).wait_send()
    wait_all(out_buf.at[pl.ds(0, grad_tiles - 1)], out_buf.at[pl.ds(0, grad_tiles - 1)], 4)
    for t in range(grad_tiles):
        i, h = t // halves, t % halves
        wgrad_ref[i * TILE_ROWS : (i + 1) * TILE_ROWS, h * LANES : (h + 1) * LANES] = out_buf[t]


def solution(mesh):
    row_count = mesh.shape["row"]
    col_count = mesh.shape["col"]
    device_count = row_count * col_count

    def body(features, weight, bias, cotangent, tile_values, tile_pos, tile_count, block_perm):
        max_tiles, tile = tile_values.shape[2], tile_values.shape[3]
        row_tiles = block_perm.shape[0] // row_count
        col_tiles = block_perm.shape[0] // col_count
        feat_rows, feat_width = features.shape
        own_rows, hidden_width = cotangent.shape
        grad_tiles = feat_width * hidden_width // (TILE_ROWS * LANES)
        vmem = pl.BlockSpec(memory_space=pltpu.VMEM)
        smem = pl.BlockSpec(memory_space=pltpu.SMEM)
        hidden, weight_grad, bias_grad = pl.pallas_call(
            functools.partial(kernel, row_count, col_count),
            out_shape=(
                jax.ShapeDtypeStruct((own_rows, hidden_width), BF16),
                jax.ShapeDtypeStruct((feat_width, hidden_width), F32),
                jax.ShapeDtypeStruct((1, hidden_width), F32),
            ),
            in_specs=[vmem, vmem, vmem, vmem, pl.BlockSpec(memory_space=pl.ANY), vmem, smem, smem],
            out_specs=(vmem, vmem, vmem),
            scratch_shapes=[
                pltpu.VMEM((max_tiles + 1, tile, tile), BF16),
                pltpu.VMEM((row_tiles * tile, col_tiles * tile), BF16),
                pltpu.VMEM((8, row_tiles * col_tiles), jnp.int32),
                pltpu.SMEM((8, row_tiles * col_tiles), jnp.int32),
                pltpu.VMEM((row_count, feat_rows, feat_width), BF16),
                pltpu.VMEM((col_tiles * tile, feat_width), BF16),
                pltpu.VMEM((row_count, col_tiles, tile), F32),
                pltpu.VMEM((col_count, 8, own_rows), F32),
                pltpu.VMEM((col_count, 8, own_rows), F32),
                pltpu.VMEM((col_count - 1, own_rows, feat_width), WIRE),
                pltpu.VMEM((col_count, own_rows, feat_width), WIRE),
                pltpu.VMEM((grad_tiles, 2 * TILE_ROWS, LANES), BF16),
                pltpu.VMEM((device_count, 2 * TILE_ROWS, LANES), BF16),
                pltpu.VMEM((grad_tiles, TILE_ROWS, LANES), F32),
                pltpu.SemaphoreType.DMA,
                pltpu.SemaphoreType.DMA,
                pltpu.SemaphoreType.DMA((row_count,)),
                pltpu.SemaphoreType.DMA((row_count,)),
                pltpu.SemaphoreType.DMA((5,)),
                pltpu.SemaphoreType.DMA((5,)),
            ],
            compiler_params=pltpu.CompilerParams(
                collective_id=0, has_side_effects=True, vmem_limit_bytes=40 * 1024 * 1024
            ),
        )(
            features,
            weight,
            bias.reshape(1, hidden_width),
            cotangent,
            tile_values,
            tile_pos,
            tile_count,
            block_perm,
        )
        return hidden, weight_grad, bias_grad.reshape(hidden_width)

    return jax.shard_map(
        body,
        mesh=mesh,
        in_specs=(
            P(("col", "row"), None),
            P(),
            P(),
            P(("row", "col"), None),
            P("row", "col", None, None, None),
            P("row", "col", None, None),
            P("row", "col"),
            P(),
        ),
        out_specs=(P(("row", "col"), None), P(), P()),
        check_vma=False,
    )
```

```python
import functools

import jax
import jax.numpy as jnp
from jax import lax
from jax.experimental import pallas as pl
from jax.experimental.pallas import tpu as pltpu
from jax.sharding import PartitionSpec as P

MESH = pl.DeviceIdType.MESH
F32 = jnp.float32
BF16 = jnp.bfloat16
WIRE = jnp.bfloat16
TILE_ROWS = 8
LANES = 128
VMEM_BYTES = 64 * 1024 * 1024


def flip(index, bits):
    place = 1
    while place <= bits:
        if (bits // place) % 2:
            index = index + place - 2 * place * lax.rem(index // place, 2)
        place *= 2
    return index


def kernel(
    row_count,
    col_count,
    feat_hbm,
    weight_hbm,
    bias_hbm,
    cot_hbm,
    tiles_hbm,
    pos_hbm,
    count_hbm,
    perm_hbm,
    hidden_out,
    wgrad_out,
    bgrad_out,
    hidden_ref,
    wgrad_ref,
    bgrad_ref,
    weight_ref,
    bias_ref,
    cot_ref,
    pos_ref,
    count_ref,
    perm_ref,
    tiles,
    dense,
    index_vmem,
    index_smem,
    gathered,
    col_part,
    col_sibling,
    col_buf,
    col_scale,
    row_sums,
    row_send,
    row_buf,
    product,
    prod_send,
    prod_buf,
    grad_send,
    grad_sibling,
    chip_send,
    chip_buf,
    out_buf,
    load_sem,
    store_sem,
    index_sem,
    feat_send_sem,
    feat_recv_sem,
    send_sem,
    recv_sem,
):
    row = lax.axis_index("row")
    col = lax.axis_index("col")
    core = lax.rem(row, 2)
    level = row // 2
    levels = row_count // 2
    chip = level * col_count + col
    chips = levels * col_count
    sibling = row + 1 - 2 * core
    max_tiles = tiles.shape[0] - 1
    tile = tiles.shape[1]
    row_tiles = dense.shape[0] // tile
    col_tiles = dense.shape[1] // tile
    own_rows = hidden_ref.shape[0]
    feat_rows = gathered.shape[1]
    hidden_width = weight_ref.shape[1]
    grad_tiles = out_buf.shape[0]
    core_tiles = grad_tiles // 2
    halves = hidden_width // LANES

    barrier = pltpu.get_barrier_semaphore()

    def greet(step, carry):
        other = lax.rem(chip + step, chips)
        pl.semaphore_signal(
            barrier,
            inc=1,
            device_id=(other // col_count * 2 + core, lax.rem(other, col_count)),
            device_id_type=MESH,
        )
        return carry

    pl.semaphore_signal(barrier, inc=1, device_id=(sibling, col), device_id_type=MESH)
    lax.fori_loop(1, chips, greet, 0)

    loads = [
        pltpu.make_async_copy(source, target, load_sem.at[i])
        for i, (source, target) in enumerate(
            (
                (feat_hbm, gathered.at[row]),
                (pos_hbm.at[0, 0], pos_ref),
                (count_hbm, count_ref),
                (perm_hbm, perm_ref),
                (tiles_hbm.at[0, 0], tiles.at[pl.ds(0, max_tiles)]),
                (weight_hbm, weight_ref),
                (bias_hbm, bias_ref),
                (cot_hbm, cot_ref),
            )
        )
    ]
    for load in loads:
        load.start()
    tiles[max_tiles] = jnp.zeros((tile, tile), BF16)
    for load in loads[1:4]:
        load.wait()

    tile_row = pos_ref[0:1, :]
    tile_col = pos_ref[1:2, :]
    code_row = jnp.zeros((1, max_tiles), jnp.int32)
    for i in range(row_tiles):
        place = perm_ref[row * row_tiles + i] - row * row_tiles
        code_row = jnp.where(tile_row == i, place, code_row)
    code_col = jnp.zeros((1, max_tiles), jnp.int32)
    for j in range(col_tiles):
        place = perm_ref[col * col_tiles + j] - col * col_tiles
        code_col = jnp.where(tile_col == j, place, code_col)
    slot_lane = lax.broadcasted_iota(jnp.int32, (1, max_tiles), 1)
    code = jnp.where(slot_lane < count_ref[0, 0], code_row * col_tiles + code_col, -1)
    code = jnp.transpose(jnp.broadcast_to(code, (LANES, max_tiles)))
    positions = row_tiles * col_tiles
    slot_sub = lax.broadcasted_iota(jnp.int32, (max_tiles, LANES), 0)
    for start in range(0, positions, LANES):
        place = lax.broadcasted_iota(jnp.int32, (max_tiles, LANES), 1) + start
        slot = jnp.min(jnp.where(code == place, slot_sub, max_tiles), axis=0, keepdims=True)
        index_vmem[:, start : start + LANES] = jnp.broadcast_to(slot, (8, LANES))
    index_copy = pltpu.make_async_copy(index_vmem, index_smem, index_sem)
    index_copy.start()

    loads[0].wait()
    pl.semaphore_wait(barrier, chips)

    def feat_copy(source_row, target_row, send_slot):
        return pltpu.make_async_remote_copy(
            src_ref=gathered.at[source_row],
            dst_ref=gathered.at[source_row],
            send_sem=feat_send_sem.at[send_slot],
            recv_sem=feat_recv_sem.at[source_row],
            device_id=(target_row, col),
            device_id_type=MESH,
        )

    for step in range(1, levels):
        feat_copy(row, flip(level, step) * 2 + core, step).start()
    feat_copy(row, sibling, 0).start()

    index_copy.wait()
    loads[4].wait()

    def build(b, carry):
        columns = pl.ds(pl.multiple_of(b * tile, tile), tile)
        total = jnp.zeros((tile, tile), F32)
        for a in range(row_tiles):
            block = tiles[index_smem[0, a * col_tiles + b]]
            dense[a * tile : (a + 1) * tile, columns] = block
            total = total + block.astype(F32)
        col_part[pl.ds(b, 1), :] = jnp.sum(total, axis=0, keepdims=True)
        return carry

    lax.fori_loop(0, col_tiles, build, 0)

    def remote(source, target_ref, target_row, target_col, which):
        return pltpu.make_async_remote_copy(
            src_ref=source,
            dst_ref=target_ref,
            send_sem=send_sem.at[which],
            recv_sem=recv_sem.at[which],
            device_id=(target_row, target_col),
            device_id_type=MESH,
        )

    def wait_all(ref, which):
        copy = remote(ref, ref, sibling, col, which)
        copy.wait_send()
        copy.wait_recv()

    remote(col_part, col_sibling, sibling, col, 0).start()

    def add_rows(k, carry):
        columns = pl.ds(pl.multiple_of(k * feat_rows, feat_rows), feat_rows)
        row_sums[...] += jnp.dot(
            dense[:, columns], jnp.ones((feat_rows, LANES), BF16), preferred_element_type=F32
        )
        return carry

    row_sums[...] = jnp.zeros(row_sums.shape, F32)
    wait_all(col_part, 0)
    col_buf[level] = col_part[...] + col_sibling[...]
    for step in range(1, levels):
        target = flip(level, step) * 2 + core
        remote(col_buf.at[level], col_buf.at[level], target, col, 1).start()

    lax.fori_loop(0, row_count, add_rows, 0)
    for k in range(col_count):
        for at in range(0, own_rows, tile):
            sums = row_sums[k * own_rows + at : k * own_rows + at + tile, :]
            row_send[k, :, at : at + tile] = jnp.transpose(sums)[0:8, :]
    for step in range(1, col_count):
        target = lax.rem(col + step, col_count)
        remote(row_send.at[target], row_buf.at[col], row, target, 2).start()
    row_buf[col] = row_send[col]

    wait_all(col_buf.at[pl.ds(0, levels - 1)], 1)
    col_total = col_buf[0]
    for other in range(1, levels):
        col_total = col_total + col_buf[other]
    col_scale[...] = lax.rsqrt(1.0 + col_total)

    def multiply(source):
        parts = []
        for at in range(0, feat_rows, tile):
            scale = col_scale[pl.ds(source * (feat_rows // tile) + at // tile, 1), :]
            scale = jnp.transpose(jnp.broadcast_to(scale, (tile, tile)))
            parts.append((scale * gathered[source, at : at + tile, :].astype(F32)).astype(BF16))
        columns = pl.ds(pl.multiple_of(source * feat_rows, feat_rows), feat_rows)
        return jnp.dot(
            dense[:, columns], jnp.concatenate(parts, axis=0), preferred_element_type=F32
        )

    product[...] = multiply(row)
    feat_copy(sibling, sibling, 0).wait_recv()
    product[...] += multiply(sibling)
    for step in range(1, levels):
        source = flip(level, step) * 2 + core
        feat_copy(source, sibling, 0).wait_recv()
        feat_copy(source, sibling, levels + step - 1).start()
        product[...] += multiply(source)
    for step in range(1, levels):
        source = flip(level, step) * 2 + 1 - core
        feat_copy(source, sibling, 0).wait_recv()
        product[...] += multiply(source)

    def piece(owner):
        return product[pl.ds(pl.multiple_of(owner * own_rows, own_rows), own_rows), :]

    for step in range(1, col_count):
        target = lax.rem(col + step, col_count)
        prod_send[step - 1] = piece(target).astype(WIRE)
        remote(prod_send.at[step - 1], prod_buf.at[col], row, target, 3).start()

    wait_all(row_buf.at[pl.ds(0, col_count - 1)], 2)
    row_total = row_buf[0]
    for c in range(1, col_count):
        row_total = row_total + row_buf[c]
    row_scale = lax.rsqrt(1.0 + row_total)
    row_scale = jnp.concatenate(
        [
            jnp.transpose(
                jnp.broadcast_to(row_scale[0:1, at : at + tile], (LANES, tile))
            )
            for at in range(0, own_rows, tile)
        ],
        axis=0,
    )
    prod_buf[col] = jnp.zeros(prod_buf.shape[1:], WIRE)
    for load in loads[5:]:
        load.wait()
    wait_all(prod_buf.at[pl.ds(0, col_count - 1)], 3)
    summed = piece(col)
    for c in range(col_count):
        summed = summed + prod_buf[c].astype(F32)

    aggregated = (row_scale * summed).astype(BF16)
    preact = jnp.dot(aggregated, weight_ref[...], preferred_element_type=F32) + bias_ref[...]
    logistic = jax.nn.sigmoid(preact)
    preact_grad = (
        cot_ref[...].astype(F32) * logistic * (1.0 + preact * (1.0 - logistic))
    ).astype(BF16)
    weight_part = lax.dot_general(
        aggregated, preact_grad, (((0,), (0,)), ((), ())), preferred_element_type=F32
    )
    bias_part = jnp.sum(preact_grad.astype(F32), axis=0, keepdims=True)

    bias_rows = jnp.concatenate(
        [bias_part[:, h * LANES : (h + 1) * LANES] for h in range(halves)]
        + [jnp.zeros((TILE_ROWS - halves, LANES), F32)],
        axis=0,
    )
    for t in range(grad_tiles):
        i, h = t // halves, t % halves
        part = weight_part[i * TILE_ROWS : (i + 1) * TILE_ROWS, h * LANES : (h + 1) * LANES]
        grad_send[t] = jnp.concatenate([part, bias_rows], axis=0)
    mine = pl.ds(pl.multiple_of(core * core_tiles, core_tiles), core_tiles)
    theirs = pl.ds(pl.multiple_of((1 - core) * core_tiles, core_tiles), core_tiles)
    remote(grad_send.at[theirs], grad_sibling, sibling, col, 4).start()
    hidden_ref[...] = (preact * logistic).astype(BF16)
    hidden_store = pltpu.make_async_copy(hidden_ref, hidden_out, store_sem.at[0])
    hidden_store.start()
    wait_all(grad_sibling, 4)
    chip_send[...] = (grad_send[mine] + grad_sibling[...]).astype(BF16)

    def send_part(step, carry):
        other = lax.rem(chip + step, chips)
        remote(
            chip_send.at[lax.rem(other, core_tiles)],
            chip_buf.at[chip],
            other // col_count * 2 + core,
            lax.rem(other, col_count),
            5,
        ).start()
        return carry

    lax.fori_loop(1, chips, send_part, 0)
    own = lax.rem(chip, core_tiles)
    chip_buf[chip] = chip_send[own]
    wait_all(chip_buf.at[pl.ds(0, chips - 1)], 5)

    def add_part(d, total):
        return total + chip_buf[d].astype(F32)

    total = lax.fori_loop(
        0, chips, add_part, jnp.zeros((2 * TILE_ROWS, LANES), F32), unroll=min(chips, 16)
    )
    inverse_root = lax.rsqrt(F32(own_rows * row_count * col_count))
    total = total * inverse_root
    slot = core * core_tiles + own
    out_buf[slot] = total[0:TILE_ROWS]
    first = chip - own

    def send_total(step, carry):
        other = first + lax.rem(own + step, core_tiles)
        remote(
            out_buf.at[slot],
            out_buf.at[slot],
            other // col_count * 2 + core,
            lax.rem(other, col_count),
            6,
        ).start()
        return carry

    lax.fori_loop(1, core_tiles, send_total, 0)
    for h in range(halves):
        bgrad_ref[:, h * LANES : (h + 1) * LANES] = total[TILE_ROWS + h : TILE_ROWS + h + 1]
    bgrad_store = pltpu.make_async_copy(bgrad_ref, bgrad_out, store_sem.at[1])
    bgrad_store.start()
    for step in range(2 * levels - 1):
        feat_copy(row, sibling, step).wait_send()
    hidden_store.wait()
    bgrad_store.wait()
    wait_all(out_buf.at[pl.ds(0, core_tiles - 1)], 6)
    remote(out_buf.at[mine], out_buf.at[mine], sibling, col, 7).start()
    wait_all(out_buf.at[pl.ds(0, core_tiles)], 7)
    for t in range(grad_tiles):
        i, h = t // halves, t % halves
        wgrad_ref[i * TILE_ROWS : (i + 1) * TILE_ROWS, h * LANES : (h + 1) * LANES] = out_buf[t]
    wgrad_store = pltpu.make_async_copy(wgrad_ref, wgrad_out, store_sem.at[2])
    wgrad_store.start()
    wgrad_store.wait()


def write_out(*refs):
    count = len(refs) // 2
    sems = refs[-1]
    copies = [
        pltpu.make_async_copy(refs[i], refs[count + i], sems.at[i]) for i in range(count)
    ]
    for copy in copies:
        copy.start()
    for copy in copies:
        copy.wait()


def solution(mesh):
    row_count = mesh.shape["row"]
    col_count = mesh.shape["col"]
    device_count = row_count * col_count

    def body(features, weight, bias, cotangent, tile_values, tile_pos, tile_count, block_perm):
        max_tiles, tile = tile_values.shape[2], tile_values.shape[3]
        row_tiles = block_perm.shape[0] // row_count
        col_tiles = block_perm.shape[0] // col_count
        feat_rows, feat_width = features.shape
        own_rows, hidden_width = cotangent.shape
        grad_tiles = feat_width * hidden_width // (TILE_ROWS * LANES)
        hbm = pl.BlockSpec(memory_space=pl.ANY)
        shapes = (
            jax.ShapeDtypeStruct((own_rows, hidden_width), BF16),
            jax.ShapeDtypeStruct((feat_width, hidden_width), F32),
            jax.ShapeDtypeStruct((1, hidden_width), F32),
        )
        results = pl.pallas_call(
            functools.partial(kernel, row_count, col_count),
            out_shape=shapes,
            in_specs=[hbm] * 8,
            out_specs=(hbm, hbm, hbm),
            scratch_shapes=[
                pltpu.VMEM((own_rows, hidden_width), BF16),
                pltpu.VMEM((feat_width, hidden_width), F32),
                pltpu.VMEM((1, hidden_width), F32),
                pltpu.VMEM(weight.shape, BF16),
                pltpu.VMEM((1, hidden_width), F32),
                pltpu.VMEM(cotangent.shape, BF16),
                pltpu.VMEM(tile_pos.shape[2:], jnp.int32),
                pltpu.SMEM(tile_count.shape, jnp.int32),
                pltpu.SMEM(block_perm.shape, jnp.int32),
                pltpu.VMEM((max_tiles + 1, tile, tile), BF16),
                pltpu.VMEM((row_tiles * tile, col_tiles * tile), BF16),
                pltpu.VMEM((8, row_tiles * col_tiles), jnp.int32),
                pltpu.SMEM((8, row_tiles * col_tiles), jnp.int32),
                pltpu.VMEM((row_count, feat_rows, feat_width), BF16),
                pltpu.VMEM((col_tiles, tile), F32),
                pltpu.VMEM((col_tiles, tile), F32),
                pltpu.VMEM((row_count // 2, col_tiles, tile), F32),
                pltpu.VMEM((col_tiles, tile), F32),
                pltpu.VMEM((row_tiles * tile, LANES), F32),
                pltpu.VMEM((col_count, 8, own_rows), F32),
                pltpu.VMEM((col_count, 8, own_rows), F32),
                pltpu.VMEM((row_tiles * tile, feat_width), F32),
                pltpu.VMEM((col_count - 1, own_rows, feat_width), WIRE),
                pltpu.VMEM((col_count, own_rows, feat_width), WIRE),
                pltpu.VMEM((grad_tiles, 2 * TILE_ROWS, LANES), F32),
                pltpu.VMEM((grad_tiles // 2, 2 * TILE_ROWS, LANES), F32),
                pltpu.VMEM((grad_tiles // 2, 2 * TILE_ROWS, LANES), BF16),
                pltpu.VMEM((device_count // 2, 2 * TILE_ROWS, LANES), BF16),
                pltpu.VMEM((grad_tiles, TILE_ROWS, LANES), F32),
                pltpu.SemaphoreType.DMA((8,)),
                pltpu.SemaphoreType.DMA((3,)),
                pltpu.SemaphoreType.DMA,
                pltpu.SemaphoreType.DMA((row_count,)),
                pltpu.SemaphoreType.DMA((row_count,)),
                pltpu.SemaphoreType.DMA((8,)),
                pltpu.SemaphoreType.DMA((8,)),
            ],
            compiler_params=pltpu.CompilerParams(
                collective_id=0, has_side_effects=True, vmem_limit_bytes=VMEM_BYTES
            ),
        )(
            features,
            weight,
            bias.reshape(1, hidden_width),
            cotangent,
            tile_values,
            tile_pos,
            tile_count,
            block_perm,
        )
        hidden, weight_grad, bias_grad = pl.pallas_call(
            write_out,
            out_shape=shapes,
            in_specs=[hbm] * 3,
            out_specs=(hbm, hbm, hbm),
            scratch_shapes=[pltpu.SemaphoreType.DMA((3,))],
            compiler_params=pltpu.CompilerParams(vmem_limit_bytes=VMEM_BYTES),
        )(*results)
        return hidden, weight_grad, bias_grad.reshape(hidden_width)

    return jax.shard_map(
        body,
        mesh=mesh,
        in_specs=(
            P(("col", "row"), None),
            P(),
            P(),
            P(("row", "col"), None),
            P("row", "col", None, None, None),
            P("row", "col", None, None),
            P("row", "col"),
            P(),
        ),
        out_specs=(P(("row", "col"), None), P(), P()),
        check_vma=False,
    )
```

```python
import functools

import jax
import jax.numpy as jnp
from jax import lax
from jax.experimental import pallas as pl
from jax.experimental.pallas import tpu as pltpu
from jax.sharding import PartitionSpec as P

MESH = pl.DeviceIdType.MESH
F32 = jnp.float32
BF16 = jnp.bfloat16
WIRE = jnp.bfloat16
TILE_ROWS = 8
LANES = 128
VMEM_BYTES = 64 * 1024 * 1024


def flip(index, bits):
    place = 1
    while place <= bits:
        if (bits // place) % 2:
            index = index + place - 2 * place * lax.rem(index // place, 2)
        place *= 2
    return index


def kernel(
    row_count,
    col_count,
    feat_hbm,
    weight_hbm,
    bias_hbm,
    cot_hbm,
    tiles_hbm,
    pos_hbm,
    count_hbm,
    perm_hbm,
    hidden_out,
    wgrad_out,
    bgrad_out,
    hidden_ref,
    wgrad_ref,
    bgrad_ref,
    weight_ref,
    bias_ref,
    cot_ref,
    pos_ref,
    count_ref,
    perm_ref,
    tiles,
    dense,
    index_vmem,
    index_smem,
    gathered,
    col_part,
    col_sibling,
    col_buf,
    col_scale,
    row_sums,
    row_send,
    row_buf,
    scaled,
    prod_send,
    prod_buf,
    grad_send,
    grad_sibling,
    chip_send,
    chip_buf,
    out_buf,
    load_sem,
    store_sem,
    index_sem,
    feat_send_sem,
    feat_recv_sem,
    send_sem,
    recv_sem,
):
    row = lax.axis_index("row")
    col = lax.axis_index("col")
    core = lax.rem(row, 2)
    level = row // 2
    levels = row_count // 2
    chip = level * col_count + col
    chips = levels * col_count
    sibling = row + 1 - 2 * core
    max_tiles = tiles.shape[0] - 1
    tile = tiles.shape[1]
    row_tiles = dense.shape[0] // tile
    col_tiles = dense.shape[1] // tile
    own_rows = hidden_ref.shape[0]
    feat_rows, feat_width = gathered.shape[1:]
    hidden_width = weight_ref.shape[1]
    grad_tiles = out_buf.shape[0]
    core_tiles = grad_tiles // 2
    halves = hidden_width // LANES

    loads = [
        pltpu.make_async_copy(source, target, load_sem.at[i])
        for i, (source, target) in enumerate(
            (
                (feat_hbm, gathered.at[row]),
                (pos_hbm.at[0, 0], pos_ref),
                (count_hbm, count_ref),
                (perm_hbm, perm_ref),
                (tiles_hbm.at[0, 0], tiles.at[pl.ds(0, max_tiles)]),
                (weight_hbm, weight_ref),
                (bias_hbm, bias_ref),
                (cot_hbm, cot_ref),
            )
        )
    ]
    for load in loads:
        load.start()
    barrier = pltpu.get_barrier_semaphore()

    def greet(step, carry):
        other = lax.rem(chip + step, chips)
        pl.semaphore_signal(
            barrier,
            inc=1,
            device_id=(other // col_count * 2 + core, lax.rem(other, col_count)),
            device_id_type=MESH,
        )
        return carry

    pl.semaphore_signal(barrier, inc=1, device_id=(sibling, col), device_id_type=MESH)
    lax.fori_loop(1, chips, greet, 0)

    tiles[max_tiles] = jnp.zeros((tile, tile), BF16)
    for load in loads[1:4]:
        load.wait()

    tile_row = pos_ref[0:1, :]
    tile_col = pos_ref[1:2, :]
    code_row = jnp.zeros((1, max_tiles), jnp.int32)
    for i in range(row_tiles):
        place = perm_ref[row * row_tiles + i] - row * row_tiles
        code_row = jnp.where(tile_row == i, place, code_row)
    code_col = jnp.zeros((1, max_tiles), jnp.int32)
    for j in range(col_tiles):
        place = perm_ref[col * col_tiles + j] - col * col_tiles
        code_col = jnp.where(tile_col == j, place, code_col)
    slot_lane = lax.broadcasted_iota(jnp.int32, (1, max_tiles), 1)
    code = jnp.where(slot_lane < count_ref[0, 0], code_row * col_tiles + code_col, -1)
    code = jnp.transpose(jnp.broadcast_to(code, (LANES, max_tiles)))
    positions = row_tiles * col_tiles
    slot_sub = lax.broadcasted_iota(jnp.int32, (max_tiles, LANES), 0)
    for start in range(0, positions, LANES):
        place = lax.broadcasted_iota(jnp.int32, (max_tiles, LANES), 1) + start
        slot = jnp.min(jnp.where(code == place, slot_sub, max_tiles), axis=0, keepdims=True)
        index_vmem[:, start : start + LANES] = jnp.broadcast_to(slot, (8, LANES))
    index_copy = pltpu.make_async_copy(index_vmem, index_smem, index_sem)
    index_copy.start()

    loads[0].wait()
    pl.semaphore_wait(barrier, chips)

    def feat_copy(source_row, target_row, send_slot):
        return pltpu.make_async_remote_copy(
            src_ref=gathered.at[source_row],
            dst_ref=gathered.at[source_row],
            send_sem=feat_send_sem.at[send_slot],
            recv_sem=feat_recv_sem.at[source_row],
            device_id=(target_row, col),
            device_id_type=MESH,
        )

    for step in range(1, levels):
        feat_copy(row, flip(level, step) * 2 + core, step).start()
    feat_copy(row, sibling, 0).start()

    index_copy.wait()
    loads[4].wait()

    def build(b, carry):
        columns = pl.ds(pl.multiple_of(b * tile, tile), tile)
        total = jnp.zeros((tile, tile), F32)
        for a in range(row_tiles):
            block = tiles[index_smem[0, a * col_tiles + b]]
            dense[a * tile : (a + 1) * tile, columns] = block
            total = total + block.astype(F32)
        col_part[pl.ds(b, 1), :] = jnp.sum(total, axis=0, keepdims=True)
        return carry

    lax.fori_loop(0, col_tiles, build, 0)

    def remote(source, target_ref, target_row, target_col, which):
        return pltpu.make_async_remote_copy(
            src_ref=source,
            dst_ref=target_ref,
            send_sem=send_sem.at[which],
            recv_sem=recv_sem.at[which],
            device_id=(target_row, target_col),
            device_id_type=MESH,
        )

    def wait_all(ref, which):
        copy = remote(ref, ref, sibling, col, which)
        copy.wait_send()
        copy.wait_recv()

    remote(col_part, col_sibling, sibling, col, 0).start()

    depth = 2 * feat_rows

    def add_rows(k, carry):
        columns = pl.ds(pl.multiple_of(k * depth, depth), depth)
        row_sums[...] += jnp.dot(
            dense[:, columns], jnp.ones((depth, LANES), BF16), preferred_element_type=F32
        )
        return carry

    row_sums[...] = jnp.zeros(row_sums.shape, F32)
    wait_all(col_part, 0)
    col_buf[level] = col_part[...] + col_sibling[...]
    for step in range(1, levels):
        target = flip(level, step) * 2 + core
        remote(col_buf.at[level], col_buf.at[level], target, col, 1).start()

    lax.fori_loop(0, row_count // 2, add_rows, 0)
    for k in range(col_count):
        for at in range(0, own_rows, tile):
            sums = row_sums[k * own_rows + at : k * own_rows + at + tile, :]
            row_send[k, :, at : at + tile] = jnp.transpose(sums)[0:8, :]
    for step in range(1, col_count):
        target = lax.rem(col + step, col_count)
        remote(row_send.at[target], row_buf.at[col], row, target, 2).start()
    row_buf[col] = row_send[col]

    for step in range(1, levels):
        source = flip(level, step) * 2 + core
        feat_copy(source, sibling, 0).wait_recv()
        feat_copy(source, sibling, levels + step - 1).start()

    wait_all(col_buf.at[pl.ds(0, levels - 1)], 1)
    col_total = col_buf[0]
    for other in range(1, levels):
        col_total = col_total + col_buf[other]
    scale = jnp.concatenate(
        [lax.rsqrt(1.0 + col_total), jnp.zeros((LANES - col_tiles, tile), F32)], axis=0
    )
    scale = jnp.transpose(scale)
    for j in range(col_tiles):
        col_scale[j] = jnp.broadcast_to(scale[:, j : j + 1], (tile, feat_width))

    def scale_rows(source):
        for i in range(feat_rows // tile):
            j = source * (feat_rows // tile) + i
            block = gathered[source, i * tile : (i + 1) * tile, :].astype(F32)
            rows = pl.ds(pl.multiple_of(j * tile, tile), tile)
            scaled[rows, :] = (col_scale[j] * block).astype(BF16)

    for step in range(levels):
        scale_rows(flip(level, step) * 2 + core)
    feat_copy(sibling, sibling, 0).wait_recv()
    for step in range(1, levels):
        feat_copy(flip(level, step) * 2 + 1 - core, sibling, 0).wait_recv()
    for step in range(levels):
        scale_rows(flip(level, step) * 2 + 1 - core)

    def piece(owner):
        rows = pl.ds(pl.multiple_of(owner * own_rows, own_rows), own_rows)
        return jnp.dot(dense[rows, :], scaled[...], preferred_element_type=F32)

    for step in range(1, col_count):
        target = lax.rem(col + step, col_count)
        prod_send[step - 1] = piece(target).astype(WIRE)
        remote(prod_send.at[step - 1], prod_buf.at[col], row, target, 3).start()
    summed = piece(col)

    wait_all(row_buf.at[pl.ds(0, col_count - 1)], 2)
    row_total = row_buf[0]
    for c in range(1, col_count):
        row_total = row_total + row_buf[c]
    row_scale = lax.rsqrt(1.0 + row_total)
    row_scale = jnp.concatenate(
        [
            jnp.transpose(
                jnp.broadcast_to(row_scale[0:1, at : at + tile], (LANES, tile))
            )
            for at in range(0, own_rows, tile)
        ],
        axis=0,
    )
    prod_buf[col] = jnp.zeros(prod_buf.shape[1:], WIRE)
    for load in loads[5:]:
        load.wait()
    wait_all(prod_buf.at[pl.ds(0, col_count - 1)], 3)
    for c in range(col_count):
        summed = summed + prod_buf[c].astype(F32)

    aggregated = (row_scale * summed).astype(BF16)
    preact = jnp.dot(aggregated, weight_ref[...], preferred_element_type=F32) + bias_ref[...]
    logistic = jax.nn.sigmoid(preact)
    preact_grad = (
        cot_ref[...].astype(F32) * logistic * (1.0 + preact * (1.0 - logistic))
    ).astype(BF16)
    weight_part = lax.dot_general(
        aggregated, preact_grad, (((0,), (0,)), ((), ())), preferred_element_type=F32
    )
    bias_part = jnp.sum(preact_grad.astype(F32), axis=0, keepdims=True)

    bias_rows = jnp.concatenate(
        [bias_part[:, h * LANES : (h + 1) * LANES] for h in range(halves)]
        + [jnp.zeros((TILE_ROWS - halves, LANES), F32)],
        axis=0,
    )
    for t in range(grad_tiles):
        i, h = t // halves, t % halves
        part = weight_part[i * TILE_ROWS : (i + 1) * TILE_ROWS, h * LANES : (h + 1) * LANES]
        grad_send[t] = jnp.concatenate([part, bias_rows], axis=0)
    mine = pl.ds(pl.multiple_of(core * core_tiles, core_tiles), core_tiles)
    theirs = pl.ds(pl.multiple_of((1 - core) * core_tiles, core_tiles), core_tiles)
    remote(grad_send.at[theirs], grad_sibling, sibling, col, 4).start()
    hidden_ref[...] = (preact * logistic).astype(BF16)
    hidden_store = pltpu.make_async_copy(hidden_ref, hidden_out, store_sem.at[0])
    hidden_store.start()
    wait_all(grad_sibling, 4)
    chip_send[...] = (grad_send[mine] + grad_sibling[...]).astype(BF16)

    def send_part(step, carry):
        other = lax.rem(chip + step, chips)
        remote(
            chip_send.at[lax.rem(other, core_tiles)],
            chip_buf.at[chip],
            other // col_count * 2 + core,
            lax.rem(other, col_count),
            5,
        ).start()
        return carry

    lax.fori_loop(1, chips, send_part, 0)
    own = lax.rem(chip, core_tiles)
    chip_buf[chip] = chip_send[own]
    wait_all(chip_buf.at[pl.ds(0, chips - 1)], 5)

    def add_part(d, total):
        return total + chip_buf[d].astype(F32)

    total = lax.fori_loop(
        0, chips, add_part, jnp.zeros((2 * TILE_ROWS, LANES), F32), unroll=min(chips, 16)
    )
    inverse_root = lax.rsqrt(F32(own_rows * row_count * col_count))
    total = total * inverse_root
    slot = core * core_tiles + own
    out_buf[slot] = total[0:TILE_ROWS]
    first = chip - own

    def send_total(step, carry):
        other = first + lax.rem(own + step, core_tiles)
        remote(
            out_buf.at[slot],
            out_buf.at[slot],
            other // col_count * 2 + core,
            lax.rem(other, col_count),
            6,
        ).start()
        return carry

    lax.fori_loop(1, core_tiles, send_total, 0)
    for h in range(halves):
        bgrad_ref[:, h * LANES : (h + 1) * LANES] = total[TILE_ROWS + h : TILE_ROWS + h + 1]
    bgrad_store = pltpu.make_async_copy(bgrad_ref, bgrad_out, store_sem.at[1])
    bgrad_store.start()
    for step in range(2 * levels - 1):
        feat_copy(row, sibling, step).wait_send()
    hidden_store.wait()
    bgrad_store.wait()
    wait_all(out_buf.at[pl.ds(0, core_tiles - 1)], 6)
    remote(out_buf.at[mine], out_buf.at[mine], sibling, col, 7).start()
    wait_all(out_buf.at[pl.ds(0, core_tiles)], 7)
    for t in range(grad_tiles):
        i, h = t // halves, t % halves
        wgrad_ref[i * TILE_ROWS : (i + 1) * TILE_ROWS, h * LANES : (h + 1) * LANES] = out_buf[t]
    wgrad_store = pltpu.make_async_copy(wgrad_ref, wgrad_out, store_sem.at[2])
    wgrad_store.start()
    wgrad_store.wait()


def write_out(*refs):
    ins, outs, held, sems = refs[0:3], refs[3:6], refs[6:9], refs[9]
    loads = [pltpu.make_async_copy(ins[i], held[i], sems.at[0, i]) for i in range(3)]
    stores = [pltpu.make_async_copy(held[i], outs[i], sems.at[1, i]) for i in range(3)]
    for load in loads:
        load.start()
    for load, store in zip(loads, stores):
        load.wait()
        store.start()
    for store in stores:
        store.wait()


def solution(mesh):
    row_count = mesh.shape["row"]
    col_count = mesh.shape["col"]
    device_count = row_count * col_count

    def body(features, weight, bias, cotangent, tile_values, tile_pos, tile_count, block_perm):
        max_tiles, tile = tile_values.shape[2], tile_values.shape[3]
        row_tiles = block_perm.shape[0] // row_count
        col_tiles = block_perm.shape[0] // col_count
        feat_rows, feat_width = features.shape
        own_rows, hidden_width = cotangent.shape
        grad_tiles = feat_width * hidden_width // (TILE_ROWS * LANES)
        hbm = pl.BlockSpec(memory_space=pl.ANY)
        shapes = (
            jax.ShapeDtypeStruct((own_rows, hidden_width), BF16),
            jax.ShapeDtypeStruct((feat_width, hidden_width), F32),
            jax.ShapeDtypeStruct((1, hidden_width), F32),
        )
        results = pl.pallas_call(
            functools.partial(kernel, row_count, col_count),
            out_shape=shapes,
            in_specs=[hbm] * 8,
            out_specs=(hbm, hbm, hbm),
            scratch_shapes=[
                pltpu.VMEM((own_rows, hidden_width), BF16),
                pltpu.VMEM((feat_width, hidden_width), F32),
                pltpu.VMEM((1, hidden_width), F32),
                pltpu.VMEM(weight.shape, BF16),
                pltpu.VMEM((1, hidden_width), F32),
                pltpu.VMEM(cotangent.shape, BF16),
                pltpu.VMEM(tile_pos.shape[2:], jnp.int32),
                pltpu.SMEM(tile_count.shape, jnp.int32),
                pltpu.SMEM(block_perm.shape, jnp.int32),
                pltpu.VMEM((max_tiles + 1, tile, tile), BF16),
                pltpu.VMEM((row_tiles * tile, col_tiles * tile), BF16),
                pltpu.VMEM((8, row_tiles * col_tiles), jnp.int32),
                pltpu.SMEM((8, row_tiles * col_tiles), jnp.int32),
                pltpu.VMEM((row_count, feat_rows, feat_width), BF16),
                pltpu.VMEM((col_tiles, tile), F32),
                pltpu.VMEM((col_tiles, tile), F32),
                pltpu.VMEM((row_count // 2, col_tiles, tile), F32),
                pltpu.VMEM((col_tiles, tile, feat_width), F32),
                pltpu.VMEM((row_tiles * tile, LANES), F32),
                pltpu.VMEM((col_count, 8, own_rows), F32),
                pltpu.VMEM((col_count, 8, own_rows), F32),
                pltpu.VMEM((col_tiles * tile, feat_width), BF16),
                pltpu.VMEM((col_count - 1, own_rows, feat_width), WIRE),
                pltpu.VMEM((col_count, own_rows, feat_width), WIRE),
                pltpu.VMEM((grad_tiles, 2 * TILE_ROWS, LANES), F32),
                pltpu.VMEM((grad_tiles // 2, 2 * TILE_ROWS, LANES), F32),
                pltpu.VMEM((grad_tiles // 2, 2 * TILE_ROWS, LANES), BF16),
                pltpu.VMEM((device_count // 2, 2 * TILE_ROWS, LANES), BF16),
                pltpu.VMEM((grad_tiles, TILE_ROWS, LANES), F32),
                pltpu.SemaphoreType.DMA((8,)),
                pltpu.SemaphoreType.DMA((3,)),
                pltpu.SemaphoreType.DMA,
                pltpu.SemaphoreType.DMA((row_count,)),
                pltpu.SemaphoreType.DMA((row_count,)),
                pltpu.SemaphoreType.DMA((8,)),
                pltpu.SemaphoreType.DMA((8,)),
            ],
            compiler_params=pltpu.CompilerParams(
                collective_id=0, has_side_effects=True, vmem_limit_bytes=VMEM_BYTES
            ),
        )(
            features,
            weight,
            bias.reshape(1, hidden_width),
            cotangent,
            tile_values,
            tile_pos,
            tile_count,
            block_perm,
        )
        hidden, weight_grad, bias_grad = pl.pallas_call(
            write_out,
            out_shape=shapes,
            in_specs=[hbm] * 3,
            out_specs=(hbm, hbm, hbm),
            scratch_shapes=[
                *(pltpu.VMEM(shape.shape, shape.dtype) for shape in shapes),
                pltpu.SemaphoreType.DMA((2, 3)),
            ],
            compiler_params=pltpu.CompilerParams(vmem_limit_bytes=VMEM_BYTES),
        )(*results)
        return hidden, weight_grad, bias_grad.reshape(hidden_width)

    return jax.shard_map(
        body,
        mesh=mesh,
        in_specs=(
            P(("col", "row"), None),
            P(),
            P(),
            P(("row", "col"), None),
            P("row", "col", None, None, None),
            P("row", "col", None, None),
            P("row", "col"),
            P(),
        ),
        out_specs=(P(("row", "col"), None), P(), P()),
        check_vma=False,
    )
```

```python
import functools

import jax
import jax.numpy as jnp
from jax import lax
from jax.experimental import pallas as pl
from jax.experimental.pallas import tpu as pltpu
from jax.sharding import PartitionSpec as P

MESH = pl.DeviceIdType.MESH
F32 = jnp.float32
BF16 = jnp.bfloat16
WIRE = jnp.bfloat16
TILE_ROWS = 8
LANES = 128
VMEM_BYTES = 48 * 1024 * 1024


def flip(index, bits):
    place = 1
    while place <= bits:
        if (bits // place) % 2:
            index = index + place - 2 * place * lax.rem(index // place, 2)
        place *= 2
    return index


def kernel(
    row_count,
    col_count,
    feat_hbm,
    weight_hbm,
    bias_hbm,
    cot_hbm,
    tiles_hbm,
    pos_hbm,
    count_hbm,
    perm_hbm,
    hidden_ref,
    wgrad_ref,
    bgrad_ref,
    weight_ref,
    bias_ref,
    cot_ref,
    pos_ref,
    count_ref,
    perm_ref,
    tiles,
    dense,
    index_vmem,
    index_smem,
    gathered,
    col_part,
    col_sibling,
    col_buf,
    col_scale,
    row_sums,
    row_send,
    row_buf,
    scaled,
    prod_send,
    prod_buf,
    grad_send,
    grad_sibling,
    chip_send,
    chip_buf,
    out_buf,
    load_sem,
    index_sem,
    feat_send_sem,
    feat_recv_sem,
    send_sem,
    recv_sem,
):
    row = lax.axis_index("row")
    col = lax.axis_index("col")
    core = lax.rem(row, 2)
    level = row // 2
    levels = row_count // 2
    chip = level * col_count + col
    chips = levels * col_count
    sibling = row + 1 - 2 * core
    level_flips = [flip(level, step) for step in range(levels)]
    col_flips = [flip(col, step) for step in range(col_count)]
    others = [
        (level_flips[step // col_count], col_flips[step % col_count]) for step in range(1, chips)
    ]
    max_tiles = tiles.shape[0] - 1
    tile = tiles.shape[1]
    row_tiles = dense.shape[0] // tile
    col_tiles = dense.shape[1] // tile
    own_rows = hidden_ref.shape[0]
    feat_rows, feat_width = gathered.shape[1:]
    hidden_width = weight_ref.shape[1]
    grad_tiles = out_buf.shape[0]
    core_tiles = grad_tiles // 2
    halves = hidden_width // LANES

    loads = [
        pltpu.make_async_copy(source, target, load_sem.at[i])
        for i, (source, target) in enumerate(
            (
                (feat_hbm, gathered.at[row]),
                (pos_hbm.at[0, 0], pos_ref),
                (count_hbm, count_ref),
                (perm_hbm, perm_ref),
                (tiles_hbm.at[0, 0], tiles.at[pl.ds(0, max_tiles)]),
                (weight_hbm, weight_ref),
                (bias_hbm, bias_ref),
                (cot_hbm, cot_ref),
            )
        )
    ]
    for load in loads:
        load.start()
    barrier = pltpu.get_barrier_semaphore()

    pl.semaphore_signal(barrier, inc=1, device_id=(sibling, col), device_id_type=MESH)
    for other_level, other_col in others:
        pl.semaphore_signal(
            barrier,
            inc=1,
            device_id=(other_level * 2 + core, other_col),
            device_id_type=MESH,
        )
    tiles[max_tiles] = jnp.zeros((tile, tile), BF16)
    for load in loads[1:4]:
        load.wait()

    tile_row = pos_ref[0:1, :]
    tile_col = pos_ref[1:2, :]
    code_row = jnp.zeros((1, max_tiles), jnp.int32)
    for i in range(row_tiles):
        place = perm_ref[row * row_tiles + i] - row * row_tiles
        code_row = jnp.where(tile_row == i, place, code_row)
    code_col = jnp.zeros((1, max_tiles), jnp.int32)
    for j in range(col_tiles):
        place = perm_ref[col * col_tiles + j] - col * col_tiles
        code_col = jnp.where(tile_col == j, place, code_col)
    slot_lane = lax.broadcasted_iota(jnp.int32, (1, max_tiles), 1)
    code = jnp.where(slot_lane < count_ref[0, 0], code_row * col_tiles + code_col, -1)
    code = jnp.transpose(jnp.broadcast_to(code, (LANES, max_tiles)))
    positions = row_tiles * col_tiles
    slot_sub = lax.broadcasted_iota(jnp.int32, (max_tiles, LANES), 0)
    for start in range(0, positions, LANES):
        place = lax.broadcasted_iota(jnp.int32, (max_tiles, LANES), 1) + start
        slot = jnp.min(jnp.where(code == place, slot_sub, max_tiles), axis=0, keepdims=True)
        index_vmem[:, start : start + LANES] = jnp.broadcast_to(slot, (8, LANES))
    index_copy = pltpu.make_async_copy(index_vmem, index_smem, index_sem)
    index_copy.start()

    loads[0].wait()
    pl.semaphore_wait(barrier, chips)

    def feat_copy(source_row, target_row, send_slot):
        return pltpu.make_async_remote_copy(
            src_ref=gathered.at[source_row],
            dst_ref=gathered.at[source_row],
            send_sem=feat_send_sem.at[send_slot],
            recv_sem=feat_recv_sem.at[source_row],
            device_id=(target_row, col),
            device_id_type=MESH,
        )

    for step in range(1, levels):
        feat_copy(row, level_flips[step] * 2 + core, step).start()
    feat_copy(row, sibling, 0).start()

    index_copy.wait()
    loads[4].wait()

    def build(b, carry):
        columns = pl.ds(pl.multiple_of(b * tile, tile), tile)
        total = jnp.zeros((tile, tile), F32)
        for a in range(row_tiles):
            block = tiles[index_smem[0, a * col_tiles + b]]
            dense[a * tile : (a + 1) * tile, columns] = block
            total = total + block.astype(F32)
        col_part[pl.ds(b, 1), :] = jnp.sum(total, axis=0, keepdims=True)
        return carry

    lax.fori_loop(0, col_tiles, build, 0)

    def remote(source, target_ref, target_row, target_col, which):
        return pltpu.make_async_remote_copy(
            src_ref=source,
            dst_ref=target_ref,
            send_sem=send_sem.at[which],
            recv_sem=recv_sem.at[which],
            device_id=(target_row, target_col),
            device_id_type=MESH,
        )

    def wait_all(ref, which):
        copy = remote(ref, ref, sibling, col, which)
        copy.wait_send()
        copy.wait_recv()

    remote(col_part, col_sibling, sibling, col, 0).start()

    depth = 2 * feat_rows

    def add_rows(k, carry):
        columns = pl.ds(pl.multiple_of(k * depth, depth), depth)
        row_sums[...] += jnp.dot(
            dense[:, columns], jnp.ones((depth, LANES), BF16), preferred_element_type=F32
        )
        return carry

    row_sums[...] = jnp.zeros(row_sums.shape, F32)
    wait_all(col_part, 0)
    col_buf[level] = col_part[...] + col_sibling[...]
    for step in range(1, levels):
        target = level_flips[step] * 2 + core
        remote(col_buf.at[level], col_buf.at[level], target, col, 1).start()

    lax.fori_loop(0, row_count // 2, add_rows, 0)
    for k in range(col_count):
        for at in range(0, own_rows, tile):
            sums = row_sums[k * own_rows + at : k * own_rows + at + tile, :]
            row_send[k, :, at : at + tile] = jnp.transpose(sums)[0:8, :]
    for step in range(1, col_count):
        target = col_flips[step]
        remote(row_send.at[target], row_buf.at[col], row, target, 2).start()
    row_buf[col] = row_send[col]

    for step in range(1, levels):
        source = level_flips[step] * 2 + core
        feat_copy(source, sibling, 0).wait_recv()
        feat_copy(source, sibling, levels + step - 1).start()

    wait_all(col_buf.at[pl.ds(0, levels - 1)], 1)
    col_total = col_buf[0]
    for other in range(1, levels):
        col_total = col_total + col_buf[other]
    scale = jnp.concatenate(
        [lax.rsqrt(1.0 + col_total), jnp.zeros((LANES - col_tiles, tile), F32)], axis=0
    )
    scale = jnp.transpose(scale)
    for j in range(col_tiles):
        col_scale[j] = jnp.broadcast_to(scale[:, j : j + 1], (tile, feat_width))

    def scale_rows(source):
        for i in range(feat_rows // tile):
            j = source * (feat_rows // tile) + i
            block = gathered[source, i * tile : (i + 1) * tile, :].astype(F32)
            rows = pl.ds(pl.multiple_of(j * tile, tile), tile)
            scaled[rows, :] = (col_scale[j] * block).astype(BF16)

    for step in range(levels):
        scale_rows(level_flips[step] * 2 + core)
    feat_copy(sibling, sibling, 0).wait_recv()
    for step in range(1, levels):
        feat_copy(level_flips[step] * 2 + 1 - core, sibling, 0).wait_recv()
    for step in range(levels):
        scale_rows(level_flips[step] * 2 + 1 - core)

    def piece(owner):
        rows = pl.ds(pl.multiple_of(owner * own_rows, own_rows), own_rows)
        return jnp.dot(dense[rows, :], scaled[...], preferred_element_type=F32)

    for step in reversed(range(1, col_count)):
        target = col_flips[step]
        prod_send[step - 1] = piece(target).astype(WIRE)
        remote(prod_send.at[step - 1], prod_buf.at[col], row, target, 3).start()
    summed = piece(col)

    wait_all(row_buf.at[pl.ds(0, col_count - 1)], 2)
    row_total = row_buf[0]
    for c in range(1, col_count):
        row_total = row_total + row_buf[c]
    row_scale = lax.rsqrt(1.0 + row_total)
    row_scale = jnp.concatenate(
        [
            jnp.transpose(
                jnp.broadcast_to(row_scale[0:1, at : at + tile], (LANES, tile))
            )
            for at in range(0, own_rows, tile)
        ],
        axis=0,
    )
    prod_buf[col] = jnp.zeros(prod_buf.shape[1:], WIRE)
    for load in loads[5:]:
        load.wait()
    wait_all(prod_buf.at[pl.ds(0, col_count - 1)], 3)
    for c in range(col_count):
        summed = summed + prod_buf[c].astype(F32)

    aggregated = (row_scale * summed).astype(BF16)
    preact = jnp.dot(aggregated, weight_ref[...], preferred_element_type=F32) + bias_ref[...]
    logistic = jax.nn.sigmoid(preact)
    preact_grad = (
        cot_ref[...].astype(F32) * logistic * (1.0 + preact * (1.0 - logistic))
    ).astype(BF16)
    weight_part = lax.dot_general(
        aggregated, preact_grad, (((0,), (0,)), ((), ())), preferred_element_type=F32
    )
    bias_part = jnp.sum(preact_grad.astype(F32), axis=0, keepdims=True)

    bias_rows = jnp.concatenate(
        [bias_part[:, h * LANES : (h + 1) * LANES] for h in range(halves)]
        + [jnp.zeros((TILE_ROWS - halves, LANES), F32)],
        axis=0,
    )
    for t in range(grad_tiles):
        i, h = t // halves, t % halves
        part = weight_part[i * TILE_ROWS : (i + 1) * TILE_ROWS, h * LANES : (h + 1) * LANES]
        grad_send[t] = jnp.concatenate([part, bias_rows], axis=0)
    mine = pl.ds(pl.multiple_of(core * core_tiles, core_tiles), core_tiles)
    theirs = pl.ds(pl.multiple_of((1 - core) * core_tiles, core_tiles), core_tiles)
    remote(grad_send.at[theirs], grad_sibling, sibling, col, 4).start()
    hidden_ref[...] = (preact * logistic).astype(BF16)
    wait_all(grad_sibling, 4)
    chip_send[...] = (grad_send[mine] + grad_sibling[...]).astype(BF16)

    for other_level, other_col in others:
        other = other_level * col_count + other_col
        remote(
            chip_send.at[lax.rem(other, core_tiles)],
            chip_buf.at[chip],
            other_level * 2 + core,
            other_col,
            5,
        ).start()
    own = lax.rem(chip, core_tiles)
    chip_buf[chip] = chip_send[own]
    wait_all(chip_buf.at[pl.ds(0, chips - 1)], 5)

    def add_part(d, total):
        return total + chip_buf[d].astype(F32)

    total = lax.fori_loop(
        0, chips, add_part, jnp.zeros((2 * TILE_ROWS, LANES), F32), unroll=min(chips, 16)
    )
    inverse_root = lax.rsqrt(F32(own_rows * row_count * col_count))
    total = total * inverse_root
    slot = core * core_tiles + own
    out_buf[slot] = total[0:TILE_ROWS]
    for other_level, other_col in others[: core_tiles - 1]:
        remote(
            out_buf.at[slot], out_buf.at[slot], other_level * 2 + core, other_col, 6
        ).start()
    for h in range(halves):
        bgrad_ref[:, h * LANES : (h + 1) * LANES] = total[TILE_ROWS + h : TILE_ROWS + h + 1]
    for step in range(2 * levels - 1):
        feat_copy(row, sibling, step).wait_send()
    wait_all(out_buf.at[pl.ds(0, core_tiles - 1)], 6)
    remote(out_buf.at[mine], out_buf.at[mine], sibling, col, 7).start()
    wait_all(out_buf.at[pl.ds(0, core_tiles)], 7)
    for t in range(grad_tiles):
        i, h = t // halves, t % halves
        wgrad_ref[i * TILE_ROWS : (i + 1) * TILE_ROWS, h * LANES : (h + 1) * LANES] = out_buf[t]


def write_out(*refs):
    ins, outs, sems = refs[0:3], refs[3:6], refs[6]
    stores = [pltpu.make_async_copy(ins[i], outs[i], sems.at[i]) for i in range(3)]
    for store in stores:
        store.start()
    for store in stores:
        store.wait()


def solution(mesh):
    row_count = mesh.shape["row"]
    col_count = mesh.shape["col"]
    device_count = row_count * col_count

    def body(features, weight, bias, cotangent, tile_values, tile_pos, tile_count, block_perm):
        max_tiles, tile = tile_values.shape[2], tile_values.shape[3]
        row_tiles = block_perm.shape[0] // row_count
        col_tiles = block_perm.shape[0] // col_count
        feat_rows, feat_width = features.shape
        own_rows, hidden_width = cotangent.shape
        grad_tiles = feat_width * hidden_width // (TILE_ROWS * LANES)
        hbm = pl.BlockSpec(memory_space=pl.ANY)
        vmem = pl.BlockSpec(memory_space=pltpu.VMEM)
        shapes = (
            jax.ShapeDtypeStruct((own_rows, hidden_width), BF16),
            jax.ShapeDtypeStruct((feat_width, hidden_width), F32),
            jax.ShapeDtypeStruct((1, hidden_width), F32),
        )
        results = pl.pallas_call(
            functools.partial(kernel, row_count, col_count),
            out_shape=shapes,
            in_specs=[hbm] * 8,
            out_specs=(vmem, vmem, vmem),
            scratch_shapes=[
                pltpu.VMEM(weight.shape, BF16),
                pltpu.VMEM((1, hidden_width), F32),
                pltpu.VMEM(cotangent.shape, BF16),
                pltpu.VMEM(tile_pos.shape[2:], jnp.int32),
                pltpu.SMEM(tile_count.shape, jnp.int32),
                pltpu.SMEM(block_perm.shape, jnp.int32),
                pltpu.VMEM((max_tiles + 1, tile, tile), BF16),
                pltpu.VMEM((row_tiles * tile, col_tiles * tile), BF16),
                pltpu.VMEM((8, row_tiles * col_tiles), jnp.int32),
                pltpu.SMEM((8, row_tiles * col_tiles), jnp.int32),
                pltpu.VMEM((row_count, feat_rows, feat_width), BF16),
                pltpu.VMEM((col_tiles, tile), F32),
                pltpu.VMEM((col_tiles, tile), F32),
                pltpu.VMEM((row_count // 2, col_tiles, tile), F32),
                pltpu.VMEM((col_tiles, tile, feat_width), F32),
                pltpu.VMEM((row_tiles * tile, LANES), F32),
                pltpu.VMEM((col_count, 8, own_rows), F32),
                pltpu.VMEM((col_count, 8, own_rows), F32),
                pltpu.VMEM((col_tiles * tile, feat_width), BF16),
                pltpu.VMEM((col_count - 1, own_rows, feat_width), WIRE),
                pltpu.VMEM((col_count, own_rows, feat_width), WIRE),
                pltpu.VMEM((grad_tiles, 2 * TILE_ROWS, LANES), F32),
                pltpu.VMEM((grad_tiles // 2, 2 * TILE_ROWS, LANES), F32),
                pltpu.VMEM((grad_tiles // 2, 2 * TILE_ROWS, LANES), BF16),
                pltpu.VMEM((device_count // 2, 2 * TILE_ROWS, LANES), BF16),
                pltpu.VMEM((grad_tiles, TILE_ROWS, LANES), F32),
                pltpu.SemaphoreType.DMA((8,)),
                pltpu.SemaphoreType.DMA,
                pltpu.SemaphoreType.DMA((row_count,)),
                pltpu.SemaphoreType.DMA((row_count,)),
                pltpu.SemaphoreType.DMA((8,)),
                pltpu.SemaphoreType.DMA((8,)),
            ],
            compiler_params=pltpu.CompilerParams(
                collective_id=0, has_side_effects=True, vmem_limit_bytes=VMEM_BYTES
            ),
        )(
            *(
                pltpu.with_memory_space_constraint(operand, pltpu.HBM)
                for operand in (features, weight, bias.reshape(1, hidden_width), cotangent)
            ),
            pltpu.with_memory_space_constraint(tile_values, pltpu.HBM),
            pltpu.with_memory_space_constraint(tile_pos, pltpu.HBM),
            tile_count,
            pltpu.with_memory_space_constraint(block_perm, pltpu.HBM),
        )
        hidden, weight_grad, bias_grad = pl.pallas_call(
            write_out,
            out_shape=shapes,
            in_specs=[vmem] * 3,
            out_specs=(hbm, hbm, hbm),
            scratch_shapes=[pltpu.SemaphoreType.DMA((3,))],
        )(*results)
        return hidden, weight_grad, bias_grad.reshape(hidden_width)

    return jax.shard_map(
        body,
        mesh=mesh,
        in_specs=(
            P(("col", "row"), None),
            P(),
            P(),
            P(("row", "col"), None),
            P("row", "col", None, None, None),
            P("row", "col", None, None),
            P("row", "col"),
            P(),
        ),
        out_specs=(P(("row", "col"), None), P(), P()),
        check_vma=False,
    )
```

```python
import functools

import jax
import jax.numpy as jnp
from jax import lax
from jax.experimental import pallas as pl
from jax.experimental.pallas import tpu as pltpu
from jax.sharding import PartitionSpec as P

MESH = pl.DeviceIdType.MESH
F32 = jnp.float32
BF16 = jnp.bfloat16
WIRE = jnp.bfloat16
TILE_ROWS = 8
LANES = 128
VMEM_BYTES = 48 * 1024 * 1024


def flip(index, bits):
    place = 1
    while place <= bits:
        if (bits // place) % 2:
            index = index + place - 2 * place * lax.rem(index // place, 2)
        place *= 2
    return index


def kernel(
    row_count,
    col_count,
    feat_hbm,
    weight_hbm,
    bias_hbm,
    cot_hbm,
    tiles_hbm,
    pos_hbm,
    count_hbm,
    perm_hbm,
    hidden_ref,
    wgrad_ref,
    bgrad_ref,
    weight_ref,
    bias_ref,
    cot_ref,
    pos_ref,
    count_ref,
    perm_ref,
    tiles,
    dense,
    index_vmem,
    index_smem,
    gathered,
    col_buf,
    col_scale,
    row_sums,
    row_send,
    row_buf,
    scaled,
    prod_send,
    prod_buf,
    grad_send,
    grad_sibling,
    chip_send,
    chip_buf,
    out_buf,
    load_sem,
    index_sem,
    feat_send_sem,
    feat_recv_sem,
    send_sem,
    recv_sem,
):
    row = lax.axis_index("row")
    col = lax.axis_index("col")
    core = lax.rem(row, 2)
    level = row // 2
    levels = row_count // 2
    chip = level * col_count + col
    chips = levels * col_count
    sibling = row + 1 - 2 * core
    level_flips = [flip(level, step) for step in range(levels)]
    col_flips = [flip(col, step) for step in range(col_count)]
    others = [
        (level_flips[step // col_count], col_flips[step % col_count]) for step in range(1, chips)
    ]
    max_tiles = tiles.shape[0] - 1
    tile = tiles.shape[1]
    row_tiles = dense.shape[0] // tile
    col_tiles = dense.shape[1] // tile
    own_rows = hidden_ref.shape[0]
    feat_rows, feat_width = gathered.shape[1:]
    hidden_width = weight_ref.shape[1]
    grad_tiles = out_buf.shape[0]
    core_tiles = grad_tiles // 2
    halves = hidden_width // LANES

    loads = [
        pltpu.make_async_copy(source, target, load_sem.at[i])
        for i, (source, target) in enumerate(
            (
                (feat_hbm, gathered.at[row]),
                (pos_hbm.at[0, 0], pos_ref),
                (count_hbm, count_ref),
                (perm_hbm, perm_ref),
                (tiles_hbm.at[0, 0], tiles.at[pl.ds(0, max_tiles)]),
                (weight_hbm, weight_ref),
                (bias_hbm, bias_ref),
                (cot_hbm, cot_ref),
            )
        )
    ]
    for load in loads:
        load.start()
    barrier = pltpu.get_barrier_semaphore()

    for other_level in level_flips:
        pl.semaphore_signal(
            barrier,
            inc=1,
            device_id=(other_level * 2 + 1 - core, col),
            device_id_type=MESH,
        )
    for other_level, other_col in others:
        pl.semaphore_signal(
            barrier,
            inc=1,
            device_id=(other_level * 2 + core, other_col),
            device_id_type=MESH,
        )
    tiles[max_tiles] = jnp.zeros((tile, tile), BF16)
    for load in loads[1:4]:
        load.wait()

    tile_row = pos_ref[0:1, :]
    tile_col = pos_ref[1:2, :]
    code_row = jnp.zeros((1, max_tiles), jnp.int32)
    for i in range(row_tiles):
        place = perm_ref[row * row_tiles + i] - row * row_tiles
        code_row = jnp.where(tile_row == i, place, code_row)
    code_col = jnp.zeros((1, max_tiles), jnp.int32)
    for j in range(col_tiles):
        place = perm_ref[col * col_tiles + j] - col * col_tiles
        code_col = jnp.where(tile_col == j, place, code_col)
    slot_lane = lax.broadcasted_iota(jnp.int32, (1, max_tiles), 1)
    code = jnp.where(slot_lane < count_ref[0, 0], code_row * col_tiles + code_col, -1)
    code = jnp.transpose(jnp.broadcast_to(code, (LANES, max_tiles)))
    positions = row_tiles * col_tiles
    slot_sub = lax.broadcasted_iota(jnp.int32, (max_tiles, LANES), 0)
    for start in range(0, positions, LANES):
        place = lax.broadcasted_iota(jnp.int32, (max_tiles, LANES), 1) + start
        slot = jnp.min(jnp.where(code == place, slot_sub, max_tiles), axis=0, keepdims=True)
        index_vmem[:, start : start + LANES] = jnp.broadcast_to(slot, (8, LANES))
    index_copy = pltpu.make_async_copy(index_vmem, index_smem, index_sem)
    index_copy.start()

    loads[0].wait()
    pl.semaphore_wait(barrier, chips - 1 + levels)

    def feat_copy(source_row, target_row, send_slot):
        return pltpu.make_async_remote_copy(
            src_ref=gathered.at[source_row],
            dst_ref=gathered.at[source_row],
            send_sem=feat_send_sem.at[send_slot],
            recv_sem=feat_recv_sem.at[source_row],
            device_id=(target_row, col),
            device_id_type=MESH,
        )

    for step in range(1, levels):
        feat_copy(row, level_flips[step] * 2 + core, step).start()
    feat_copy(row, sibling, 0).start()

    index_copy.wait()
    loads[4].wait()

    def build(b, carry):
        columns = pl.ds(pl.multiple_of(b * tile, tile), tile)
        total = jnp.zeros((tile, tile), F32)
        for a in range(row_tiles):
            block = tiles[index_smem[0, a * col_tiles + b]]
            dense[a * tile : (a + 1) * tile, columns] = block
            total = total + block.astype(F32)
        col_buf[row, pl.ds(b, 1), :] = jnp.sum(total, axis=0, keepdims=True)
        return carry

    lax.fori_loop(0, col_tiles, build, 0)

    def remote(source, target_ref, target_row, target_col, which):
        return pltpu.make_async_remote_copy(
            src_ref=source,
            dst_ref=target_ref,
            send_sem=send_sem.at[which],
            recv_sem=recv_sem.at[which],
            device_id=(target_row, target_col),
            device_id_type=MESH,
        )

    def wait_all(ref, which):
        copy = remote(ref, ref, sibling, col, which)
        copy.wait_send()
        copy.wait_recv()

    for other_level in level_flips[1:]:
        target = other_level * 2 + core
        remote(col_buf.at[row], col_buf.at[row], target, col, 1).start()
    for other_level in level_flips:
        target = other_level * 2 + 1 - core
        remote(col_buf.at[row], col_buf.at[row], target, col, 1).start()

    for step in range(1, levels):
        source = level_flips[step] * 2 + core
        feat_copy(source, sibling, 0).wait_recv()
        feat_copy(source, sibling, levels + step - 1).start()

    wait_all(col_buf.at[pl.ds(0, row_count - 1)], 1)
    col_total = col_buf[0]
    for other in range(1, row_count):
        col_total = col_total + col_buf[other]
    scale = jnp.concatenate(
        [lax.rsqrt(1.0 + col_total), jnp.zeros((LANES - col_tiles, tile), F32)], axis=0
    )
    scale = jnp.transpose(scale)
    for j in range(col_tiles):
        col_scale[j] = jnp.broadcast_to(scale[:, j : j + 1], (tile, feat_width))

    def scale_rows(source):
        for i in range(feat_rows // tile):
            j = source * (feat_rows // tile) + i
            block = gathered[source, i * tile : (i + 1) * tile, :].astype(F32)
            rows = pl.ds(pl.multiple_of(j * tile, tile), tile)
            scaled[rows, :] = (col_scale[j] * block).astype(BF16)

    for step in range(levels):
        scale_rows(level_flips[step] * 2 + core)
    feat_copy(sibling, sibling, 0).wait_recv()
    for step in range(1, levels):
        feat_copy(level_flips[step] * 2 + 1 - core, sibling, 0).wait_recv()
    for step in range(levels):
        scale_rows(level_flips[step] * 2 + 1 - core)

    def piece(owner):
        rows = pl.ds(pl.multiple_of(owner * own_rows, own_rows), own_rows)
        return jnp.dot(dense[rows, :], scaled[...], preferred_element_type=F32)

    for step in reversed(range(1, col_count)):
        target = col_flips[step]
        prod_send[step - 1] = piece(target).astype(WIRE)
        remote(prod_send.at[step - 1], prod_buf.at[col], row, target, 3).start()
    summed = piece(col)

    depth = 2 * feat_rows

    def add_rows(k, carry):
        columns = pl.ds(pl.multiple_of(k * depth, depth), depth)
        row_sums[...] += jnp.dot(
            dense[:, columns], jnp.ones((depth, LANES), BF16), preferred_element_type=F32
        )
        return carry

    row_sums[...] = jnp.zeros(row_sums.shape, F32)
    lax.fori_loop(0, row_count // 2, add_rows, 0)
    for k in range(col_count):
        for at in range(0, own_rows, tile):
            sums = row_sums[k * own_rows + at : k * own_rows + at + tile, :]
            row_send[k, :, at : at + tile] = jnp.transpose(sums)[0:8, :]
    for step in range(1, col_count):
        target = col_flips[step]
        remote(row_send.at[target], row_buf.at[col], row, target, 2).start()
    row_buf[col] = row_send[col]

    wait_all(row_buf.at[pl.ds(0, col_count - 1)], 2)
    row_total = row_buf[0]
    for c in range(1, col_count):
        row_total = row_total + row_buf[c]
    row_scale = lax.rsqrt(1.0 + row_total)
    row_scale = jnp.concatenate(
        [
            jnp.transpose(
                jnp.broadcast_to(row_scale[0:1, at : at + tile], (LANES, tile))
            )
            for at in range(0, own_rows, tile)
        ],
        axis=0,
    )
    prod_buf[col] = jnp.zeros(prod_buf.shape[1:], WIRE)
    for load in loads[5:]:
        load.wait()
    wait_all(prod_buf.at[pl.ds(0, col_count - 1)], 3)
    for c in range(col_count):
        summed = summed + prod_buf[c].astype(F32)

    aggregated = (row_scale * summed).astype(BF16)
    preact = jnp.dot(aggregated, weight_ref[...], preferred_element_type=F32) + bias_ref[...]
    logistic = jax.nn.sigmoid(preact)
    preact_grad = (
        cot_ref[...].astype(F32) * logistic * (1.0 + preact * (1.0 - logistic))
    ).astype(BF16)
    weight_part = lax.dot_general(
        aggregated, preact_grad, (((0,), (0,)), ((), ())), preferred_element_type=F32
    )
    bias_part = jnp.sum(preact_grad.astype(F32), axis=0, keepdims=True)

    bias_rows = jnp.concatenate(
        [bias_part[:, h * LANES : (h + 1) * LANES] for h in range(halves)]
        + [jnp.zeros((TILE_ROWS - halves, LANES), F32)],
        axis=0,
    )
    for t in range(grad_tiles):
        i, h = t // halves, t % halves
        part = weight_part[i * TILE_ROWS : (i + 1) * TILE_ROWS, h * LANES : (h + 1) * LANES]
        grad_send[t] = jnp.concatenate([part, bias_rows], axis=0)
    mine = pl.ds(pl.multiple_of(core * core_tiles, core_tiles), core_tiles)
    theirs = pl.ds(pl.multiple_of((1 - core) * core_tiles, core_tiles), core_tiles)
    remote(grad_send.at[theirs], grad_sibling, sibling, col, 4).start()
    hidden_ref[...] = (preact * logistic).astype(BF16)
    wait_all(grad_sibling, 4)
    chip_send[...] = (grad_send[mine] + grad_sibling[...]).astype(BF16)

    for other_level, other_col in others:
        other = other_level * col_count + other_col
        remote(
            chip_send.at[lax.rem(other, core_tiles)],
            chip_buf.at[chip],
            other_level * 2 + core,
            other_col,
            5,
        ).start()
    own = lax.rem(chip, core_tiles)
    chip_buf[chip] = chip_send[own]
    wait_all(chip_buf.at[pl.ds(0, chips - 1)], 5)

    def add_part(d, total):
        return total + chip_buf[d].astype(F32)

    total = lax.fori_loop(
        0, chips, add_part, jnp.zeros((2 * TILE_ROWS, LANES), F32), unroll=min(chips, 16)
    )
    inverse_root = lax.rsqrt(F32(own_rows * row_count * col_count))
    total = total * inverse_root
    slot = core * core_tiles + own
    out_buf[slot] = total[0:TILE_ROWS]
    for other_level, other_col in others[: core_tiles - 1]:
        remote(
            out_buf.at[slot], out_buf.at[slot], other_level * 2 + core, other_col, 6
        ).start()
    for h in range(halves):
        bgrad_ref[:, h * LANES : (h + 1) * LANES] = total[TILE_ROWS + h : TILE_ROWS + h + 1]
    for step in range(2 * levels - 1):
        feat_copy(row, sibling, step).wait_send()
    wait_all(out_buf.at[pl.ds(0, core_tiles - 1)], 6)
    remote(out_buf.at[mine], out_buf.at[mine], sibling, col, 7).start()
    wait_all(out_buf.at[pl.ds(0, core_tiles)], 7)
    for t in range(grad_tiles):
        i, h = t // halves, t % halves
        wgrad_ref[i * TILE_ROWS : (i + 1) * TILE_ROWS, h * LANES : (h + 1) * LANES] = out_buf[t]


def solution(mesh):
    row_count = mesh.shape["row"]
    col_count = mesh.shape["col"]
    device_count = row_count * col_count

    def body(features, weight, bias, cotangent, tile_values, tile_pos, tile_count, block_perm):
        max_tiles, tile = tile_values.shape[2], tile_values.shape[3]
        row_tiles = block_perm.shape[0] // row_count
        col_tiles = block_perm.shape[0] // col_count
        feat_rows, feat_width = features.shape
        own_rows, hidden_width = cotangent.shape
        grad_tiles = feat_width * hidden_width // (TILE_ROWS * LANES)
        hbm = pl.BlockSpec(memory_space=pl.ANY)
        vmem = pl.BlockSpec(memory_space=pltpu.VMEM)
        shapes = (
            jax.ShapeDtypeStruct((own_rows, hidden_width), BF16),
            jax.ShapeDtypeStruct((feat_width, hidden_width), F32),
            jax.ShapeDtypeStruct((1, hidden_width), F32),
        )
        hidden, weight_grad, bias_grad = pl.pallas_call(
            functools.partial(kernel, row_count, col_count),
            out_shape=shapes,
            in_specs=[hbm] * 8,
            out_specs=(vmem, vmem, vmem),
            scratch_shapes=[
                pltpu.VMEM(weight.shape, BF16),
                pltpu.VMEM((1, hidden_width), F32),
                pltpu.VMEM(cotangent.shape, BF16),
                pltpu.VMEM(tile_pos.shape[2:], jnp.int32),
                pltpu.SMEM(tile_count.shape, jnp.int32),
                pltpu.SMEM(block_perm.shape, jnp.int32),
                pltpu.VMEM((max_tiles + 1, tile, tile), BF16),
                pltpu.VMEM((row_tiles * tile, col_tiles * tile), BF16),
                pltpu.VMEM((8, row_tiles * col_tiles), jnp.int32),
                pltpu.SMEM((8, row_tiles * col_tiles), jnp.int32),
                pltpu.VMEM((row_count, feat_rows, feat_width), BF16),
                pltpu.VMEM((row_count, col_tiles, tile), F32),
                pltpu.VMEM((col_tiles, tile, feat_width), F32),
                pltpu.VMEM((row_tiles * tile, LANES), F32),
                pltpu.VMEM((col_count, 8, own_rows), F32),
                pltpu.VMEM((col_count, 8, own_rows), F32),
                pltpu.VMEM((col_tiles * tile, feat_width), BF16),
                pltpu.VMEM((col_count - 1, own_rows, feat_width), WIRE),
                pltpu.VMEM((col_count, own_rows, feat_width), WIRE),
                pltpu.VMEM((grad_tiles, 2 * TILE_ROWS, LANES), F32),
                pltpu.VMEM((grad_tiles // 2, 2 * TILE_ROWS, LANES), F32),
                pltpu.VMEM((grad_tiles // 2, 2 * TILE_ROWS, LANES), BF16),
                pltpu.VMEM((device_count // 2, 2 * TILE_ROWS, LANES), BF16),
                pltpu.VMEM((grad_tiles, TILE_ROWS, LANES), F32),
                pltpu.SemaphoreType.DMA((8,)),
                pltpu.SemaphoreType.DMA,
                pltpu.SemaphoreType.DMA((row_count,)),
                pltpu.SemaphoreType.DMA((row_count,)),
                pltpu.SemaphoreType.DMA((8,)),
                pltpu.SemaphoreType.DMA((8,)),
            ],
            compiler_params=pltpu.CompilerParams(
                collective_id=0, has_side_effects=True, vmem_limit_bytes=VMEM_BYTES
            ),
        )(
            *(
                pltpu.with_memory_space_constraint(operand, pltpu.HBM)
                for operand in (features, weight, bias.reshape(1, hidden_width), cotangent)
            ),
            pltpu.with_memory_space_constraint(tile_values, pltpu.HBM),
            pltpu.with_memory_space_constraint(tile_pos, pltpu.HBM),
            tile_count,
            pltpu.with_memory_space_constraint(block_perm, pltpu.HBM),
        )
        return hidden, weight_grad, bias_grad.reshape(hidden_width)

    return jax.shard_map(
        body,
        mesh=mesh,
        in_specs=(
            P(("col", "row"), None),
            P(),
            P(),
            P(("row", "col"), None),
            P("row", "col", None, None, None),
            P("row", "col", None, None),
            P("row", "col"),
            P(),
        ),
        out_specs=(P(("row", "col"), None), P(), P()),
        check_vma=False,
    )
```

```python
import functools

import jax
import jax.numpy as jnp
from jax import lax
from jax.experimental import pallas as pl
from jax.experimental.pallas import tpu as pltpu
from jax.sharding import PartitionSpec as P

MESH = pl.DeviceIdType.MESH
F32 = jnp.float32
BF16 = jnp.bfloat16
WIRE = jnp.bfloat16
TILE_ROWS = 8
LANES = 128
VMEM_BYTES = 48 * 1024 * 1024


def flip(index, bits):
    place = 1
    while place <= bits:
        if (bits // place) % 2:
            index = index + place - 2 * place * lax.rem(index // place, 2)
        place *= 2
    return index


def kernel(
    row_count,
    col_count,
    feat_hbm,
    weight_hbm,
    bias_hbm,
    cot_hbm,
    tiles_hbm,
    pos_hbm,
    count_hbm,
    perm_hbm,
    hidden_ref,
    wgrad_ref,
    bgrad_ref,
    weight_ref,
    bias_ref,
    cot_ref,
    pos_ref,
    count_ref,
    perm_ref,
    tiles,
    dense,
    index_vmem,
    index_smem,
    gathered,
    col_buf,
    col_scale,
    row_send,
    row_buf,
    scaled,
    prod_send,
    prod_buf,
    grad_send,
    grad_sibling,
    chip_send,
    chip_buf,
    out_buf,
    load_sem,
    index_sem,
    feat_send_sem,
    feat_recv_sem,
    send_sem,
    recv_sem,
):
    row = lax.axis_index("row")
    col = lax.axis_index("col")
    core = lax.rem(row, 2)
    level = row // 2
    levels = row_count // 2
    chip = level * col_count + col
    chips = levels * col_count
    sibling = row + 1 - 2 * core
    level_flips = [flip(level, step) for step in range(levels)]
    col_flips = [flip(col, step) for step in range(col_count)]
    others = [
        (level_flips[step // col_count], col_flips[step % col_count]) for step in range(1, chips)
    ]
    max_tiles = tiles.shape[0] - 1
    tile = tiles.shape[1]
    row_tiles = dense.shape[0] // tile
    col_tiles = dense.shape[1] // tile
    own_rows = hidden_ref.shape[0]
    feat_rows, feat_width = gathered.shape[1:]
    hidden_width = weight_ref.shape[1]
    grad_tiles = out_buf.shape[0]
    core_tiles = grad_tiles // 2
    halves = hidden_width // LANES

    loads = [
        pltpu.make_async_copy(source, target, load_sem.at[i])
        for i, (source, target) in enumerate(
            (
                (feat_hbm, gathered.at[row]),
                (pos_hbm.at[0, 0], pos_ref),
                (count_hbm, count_ref),
                (perm_hbm, perm_ref),
                (tiles_hbm.at[0, 0], tiles.at[pl.ds(0, max_tiles)]),
                (weight_hbm, weight_ref),
                (bias_hbm, bias_ref),
                (cot_hbm, cot_ref),
            )
        )
    ]
    for load in loads:
        load.start()
    barrier = pltpu.get_barrier_semaphore()

    for other_level in level_flips:
        pl.semaphore_signal(
            barrier,
            inc=1,
            device_id=(other_level * 2 + 1 - core, col),
            device_id_type=MESH,
        )
    for other_level, other_col in others:
        pl.semaphore_signal(
            barrier,
            inc=1,
            device_id=(other_level * 2 + core, other_col),
            device_id_type=MESH,
        )
    tiles[max_tiles] = jnp.zeros((tile, tile), BF16)
    for load in loads[1:4]:
        load.wait()

    tile_row = pos_ref[0:1, :]
    tile_col = pos_ref[1:2, :]
    code_row = jnp.zeros((1, max_tiles), jnp.int32)
    for i in range(row_tiles):
        place = perm_ref[row * row_tiles + i] - row * row_tiles
        code_row = jnp.where(tile_row == i, place, code_row)
    code_col = jnp.zeros((1, max_tiles), jnp.int32)
    for j in range(col_tiles):
        place = perm_ref[col * col_tiles + j] - col * col_tiles
        code_col = jnp.where(tile_col == j, place, code_col)
    slot_lane = lax.broadcasted_iota(jnp.int32, (1, max_tiles), 1)
    code = jnp.where(slot_lane < count_ref[0, 0], code_row * col_tiles + code_col, -1)
    code = jnp.transpose(jnp.broadcast_to(code, (LANES, max_tiles)))
    positions = row_tiles * col_tiles
    slot_sub = lax.broadcasted_iota(jnp.int32, (max_tiles, LANES), 0)
    for start in range(0, positions, LANES):
        place = lax.broadcasted_iota(jnp.int32, (max_tiles, LANES), 1) + start
        slot = jnp.min(jnp.where(code == place, slot_sub, max_tiles), axis=0, keepdims=True)
        index_vmem[:, start : start + LANES] = jnp.broadcast_to(slot, (8, LANES))
    index_copy = pltpu.make_async_copy(index_vmem, index_smem, index_sem)
    index_copy.start()

    loads[0].wait()
    pl.semaphore_wait(barrier, chips - 1 + levels)

    def feat_copy(source_row, target_row, send_slot):
        return pltpu.make_async_remote_copy(
            src_ref=gathered.at[source_row],
            dst_ref=gathered.at[source_row],
            send_sem=feat_send_sem.at[send_slot],
            recv_sem=feat_recv_sem.at[source_row],
            device_id=(target_row, col),
            device_id_type=MESH,
        )

    for step in range(1, levels):
        feat_copy(row, level_flips[step] * 2 + core, step).start()
    feat_copy(row, sibling, 0).start()

    index_copy.wait()
    loads[4].wait()

    def build(b, carry):
        columns = pl.ds(pl.multiple_of(b * tile, tile), tile)
        total = jnp.zeros((tile, tile), F32)
        for a in range(row_tiles):
            block = tiles[index_smem[0, a * col_tiles + b]]
            dense[a * tile : (a + 1) * tile, columns] = block
            total = total + block.astype(F32)
        col_buf[row, pl.ds(b, 1), :] = jnp.sum(total, axis=0, keepdims=True)
        return carry

    lax.fori_loop(0, col_tiles, build, 0)

    def remote(source, target_ref, target_row, target_col, which):
        return pltpu.make_async_remote_copy(
            src_ref=source,
            dst_ref=target_ref,
            send_sem=send_sem.at[which],
            recv_sem=recv_sem.at[which],
            device_id=(target_row, target_col),
            device_id_type=MESH,
        )

    def wait_all(ref, which):
        copy = remote(ref, ref, sibling, col, which)
        copy.wait_send()
        copy.wait_recv()

    for other_level in level_flips[1:]:
        target = other_level * 2 + core
        remote(col_buf.at[row], col_buf.at[row], target, col, 1).start()
    for other_level in level_flips:
        target = other_level * 2 + 1 - core
        remote(col_buf.at[row], col_buf.at[row], target, col, 1).start()

    pieces = own_rows // tile

    def add_rows(a, carry):
        rows = pl.ds(pl.multiple_of(a * tile, tile), tile)
        total = jnp.zeros((tile, tile), F32)
        for b in range(col_tiles):
            total = total + dense[rows, b * tile : (b + 1) * tile].astype(F32)
        sums = jnp.sum(jnp.transpose(total), axis=0, keepdims=True)
        row_send[a // pieces, lax.rem(a, pieces)] = jnp.broadcast_to(sums, (8, tile))
        return carry

    lax.fori_loop(0, row_tiles, add_rows, 0)
    for step in range(1, col_count):
        target = col_flips[step]
        remote(row_send.at[target], row_buf.at[col], row, target, 2).start()
    row_buf[col] = row_send[col]

    for step in range(1, levels):
        source = level_flips[step] * 2 + core
        feat_copy(source, sibling, 0).wait_recv()
        feat_copy(source, sibling, levels + step - 1).start()

    wait_all(col_buf.at[pl.ds(0, row_count - 1)], 1)
    col_total = col_buf[0]
    for other in range(1, row_count):
        col_total = col_total + col_buf[other]
    scale = jnp.concatenate(
        [lax.rsqrt(1.0 + col_total), jnp.zeros((LANES - col_tiles, tile), F32)], axis=0
    )
    scale = jnp.transpose(scale)
    for j in range(col_tiles):
        col_scale[j] = jnp.broadcast_to(scale[:, j : j + 1], (tile, feat_width))

    def scale_rows(source):
        for i in range(feat_rows // tile):
            j = source * (feat_rows // tile) + i
            block = gathered[source, i * tile : (i + 1) * tile, :].astype(F32)
            rows = pl.ds(pl.multiple_of(j * tile, tile), tile)
            scaled[rows, :] = (col_scale[j] * block).astype(BF16)

    for step in range(levels):
        scale_rows(level_flips[step] * 2 + core)
    feat_copy(sibling, sibling, 0).wait_recv()
    for step in range(1, levels):
        feat_copy(level_flips[step] * 2 + 1 - core, sibling, 0).wait_recv()
    for step in range(levels):
        scale_rows(level_flips[step] * 2 + 1 - core)

    def piece(owner):
        rows = pl.ds(pl.multiple_of(owner * own_rows, own_rows), own_rows)
        return jnp.dot(dense[rows, :], scaled[...], preferred_element_type=F32)

    for step in reversed(range(1, col_count)):
        target = col_flips[step]
        prod_send[step - 1] = piece(target).astype(WIRE)
        remote(prod_send.at[step - 1], prod_buf.at[col], row, target, 3).start()
    summed = piece(col)

    wait_all(row_buf.at[pl.ds(0, col_count - 1)], 2)
    row_total = row_buf[0]
    for c in range(1, col_count):
        row_total = row_total + row_buf[c]
    row_scale = lax.rsqrt(1.0 + row_total)
    row_scale = jnp.concatenate(
        [
            jnp.transpose(
                jnp.broadcast_to(row_scale[at, 0:1, :], (LANES, tile))
            )
            for at in range(pieces)
        ],
        axis=0,
    )
    prod_buf[col] = jnp.zeros(prod_buf.shape[1:], WIRE)
    for load in loads[5:]:
        load.wait()
    wait_all(prod_buf.at[pl.ds(0, col_count - 1)], 3)
    for c in range(col_count):
        summed = summed + prod_buf[c].astype(F32)

    aggregated = (row_scale * summed).astype(BF16)
    preact = jnp.dot(aggregated, weight_ref[...], preferred_element_type=F32) + bias_ref[...]
    logistic = jax.nn.sigmoid(preact)
    preact_grad = (
        cot_ref[...].astype(F32) * logistic * (1.0 + preact * (1.0 - logistic))
    ).astype(BF16)
    weight_part = lax.dot_general(
        aggregated, preact_grad, (((0,), (0,)), ((), ())), preferred_element_type=F32
    )
    bias_part = jnp.sum(preact_grad.astype(F32), axis=0, keepdims=True)

    bias_rows = jnp.concatenate(
        [bias_part[:, h * LANES : (h + 1) * LANES] for h in range(halves)]
        + [jnp.zeros((TILE_ROWS - halves, LANES), F32)],
        axis=0,
    )
    for t in range(grad_tiles):
        i, h = t // halves, t % halves
        part = weight_part[i * TILE_ROWS : (i + 1) * TILE_ROWS, h * LANES : (h + 1) * LANES]
        grad_send[t] = jnp.concatenate([part, bias_rows], axis=0)
    mine = pl.ds(pl.multiple_of(core * core_tiles, core_tiles), core_tiles)
    theirs = pl.ds(pl.multiple_of((1 - core) * core_tiles, core_tiles), core_tiles)
    remote(grad_send.at[theirs], grad_sibling, sibling, col, 4).start()
    hidden_ref[...] = (preact * logistic).astype(BF16)
    wait_all(grad_sibling, 4)
    chip_send[...] = (grad_send[mine] + grad_sibling[...]).astype(BF16)

    for other_level, other_col in others:
        other = other_level * col_count + other_col
        remote(
            chip_send.at[lax.rem(other, core_tiles)],
            chip_buf.at[chip],
            other_level * 2 + core,
            other_col,
            5,
        ).start()
    own = lax.rem(chip, core_tiles)
    chip_buf[chip] = chip_send[own]
    wait_all(chip_buf.at[pl.ds(0, chips - 1)], 5)

    def add_part(d, total):
        return total + chip_buf[d].astype(F32)

    total = lax.fori_loop(
        0, chips, add_part, jnp.zeros((2 * TILE_ROWS, LANES), F32), unroll=min(chips, 16)
    )
    inverse_root = lax.rsqrt(F32(own_rows * row_count * col_count))
    total = total * inverse_root
    slot = core * core_tiles + own
    out_buf[slot] = total[0:TILE_ROWS]
    for other_level, other_col in others[: core_tiles - 1]:
        remote(
            out_buf.at[slot], out_buf.at[slot], other_level * 2 + core, other_col, 6
        ).start()
    for h in range(halves):
        bgrad_ref[:, h * LANES : (h + 1) * LANES] = total[TILE_ROWS + h : TILE_ROWS + h + 1]
    for step in range(2 * levels - 1):
        feat_copy(row, sibling, step).wait_send()
    wait_all(out_buf.at[pl.ds(0, core_tiles - 1)], 6)
    remote(out_buf.at[mine], out_buf.at[mine], sibling, col, 7).start()
    wait_all(out_buf.at[pl.ds(0, core_tiles)], 7)
    for t in range(grad_tiles):
        i, h = t // halves, t % halves
        wgrad_ref[i * TILE_ROWS : (i + 1) * TILE_ROWS, h * LANES : (h + 1) * LANES] = out_buf[t]


def solution(mesh):
    row_count = mesh.shape["row"]
    col_count = mesh.shape["col"]
    device_count = row_count * col_count

    def body(features, weight, bias, cotangent, tile_values, tile_pos, tile_count, block_perm):
        max_tiles, tile = tile_values.shape[2], tile_values.shape[3]
        row_tiles = block_perm.shape[0] // row_count
        col_tiles = block_perm.shape[0] // col_count
        feat_rows, feat_width = features.shape
        own_rows, hidden_width = cotangent.shape
        grad_tiles = feat_width * hidden_width // (TILE_ROWS * LANES)
        hbm = pl.BlockSpec(memory_space=pl.ANY)
        vmem = pl.BlockSpec(memory_space=pltpu.VMEM)
        shapes = (
            jax.ShapeDtypeStruct((own_rows, hidden_width), BF16),
            jax.ShapeDtypeStruct((feat_width, hidden_width), F32),
            jax.ShapeDtypeStruct((1, hidden_width), F32),
        )
        hidden, weight_grad, bias_grad = pl.pallas_call(
            functools.partial(kernel, row_count, col_count),
            out_shape=shapes,
            in_specs=[hbm] * 8,
            out_specs=(vmem, vmem, vmem),
            scratch_shapes=[
                pltpu.VMEM(weight.shape, BF16),
                pltpu.VMEM((1, hidden_width), F32),
                pltpu.VMEM(cotangent.shape, BF16),
                pltpu.VMEM(tile_pos.shape[2:], jnp.int32),
                pltpu.SMEM(tile_count.shape, jnp.int32),
                pltpu.SMEM(block_perm.shape, jnp.int32),
                pltpu.VMEM((max_tiles + 1, tile, tile), BF16),
                pltpu.VMEM((row_tiles * tile, col_tiles * tile), BF16),
                pltpu.VMEM((8, row_tiles * col_tiles), jnp.int32),
                pltpu.SMEM((8, row_tiles * col_tiles), jnp.int32),
                pltpu.VMEM((row_count, feat_rows, feat_width), BF16),
                pltpu.VMEM((row_count, col_tiles, tile), F32),
                pltpu.VMEM((col_tiles, tile, feat_width), F32),
                pltpu.VMEM((col_count, own_rows // tile, 8, tile), F32),
                pltpu.VMEM((col_count, own_rows // tile, 8, tile), F32),
                pltpu.VMEM((col_tiles * tile, feat_width), BF16),
                pltpu.VMEM((col_count - 1, own_rows, feat_width), WIRE),
                pltpu.VMEM((col_count, own_rows, feat_width), WIRE),
                pltpu.VMEM((grad_tiles, 2 * TILE_ROWS, LANES), F32),
                pltpu.VMEM((grad_tiles // 2, 2 * TILE_ROWS, LANES), F32),
                pltpu.VMEM((grad_tiles // 2, 2 * TILE_ROWS, LANES), BF16),
                pltpu.VMEM((device_count // 2, 2 * TILE_ROWS, LANES), BF16),
                pltpu.VMEM((grad_tiles, TILE_ROWS, LANES), F32),
                pltpu.SemaphoreType.DMA((8,)),
                pltpu.SemaphoreType.DMA,
                pltpu.SemaphoreType.DMA((row_count,)),
                pltpu.SemaphoreType.DMA((row_count,)),
                pltpu.SemaphoreType.DMA((8,)),
                pltpu.SemaphoreType.DMA((8,)),
            ],
            compiler_params=pltpu.CompilerParams(
                collective_id=0, has_side_effects=True, vmem_limit_bytes=VMEM_BYTES
            ),
        )(
            *(
                pltpu.with_memory_space_constraint(operand, pltpu.HBM)
                for operand in (features, weight, bias.reshape(1, hidden_width), cotangent)
            ),
            pltpu.with_memory_space_constraint(tile_values, pltpu.HBM),
            pltpu.with_memory_space_constraint(tile_pos, pltpu.HBM),
            tile_count,
            pltpu.with_memory_space_constraint(block_perm, pltpu.HBM),
        )
        return hidden, weight_grad, bias_grad.reshape(hidden_width)

    return jax.shard_map(
        body,
        mesh=mesh,
        in_specs=(
            P(("col", "row"), None),
            P(),
            P(),
            P(("row", "col"), None),
            P("row", "col", None, None, None),
            P("row", "col", None, None),
            P("row", "col"),
            P(),
        ),
        out_specs=(P(("row", "col"), None), P(), P()),
        check_vma=False,
    )
```
